256 devices in a mesh: rows: 64 (over x, y_lo, z), cols: 4 (over y_hi, core).
Axes of the slice: x: 4, y: 4 (y_hi: 2, y_lo: 2; y = y_hi * 2 + y_lo), z: 8, core: 2. Of those that a mesh axis runs over, the one named last changes fastest.
Arguments:
- right_side: float32 [32, 131072], P(None, ('rows', 'cols')), may hold values from -6 to 6
- local_inverse: float32 [64, 4, 1024, 1024], P('rows', 'cols'), may hold values from -1 to 2.5, as said below
- modes: float32 [64, 4, 64, 1024], P('rows', 'cols'), may hold values from -0.1875 to 0.1875
- coarse_inverse: float32 [16384, 16384], P('rows', 'cols'), may hold values from -1 to 2.5, as said below
- stiff_diag: float32 [64, 4, 1024], P('rows', 'cols'), may hold values from 1 to 4
- nbr_index: int32 [64, 4, 80, 1024], P('rows', 'cols'), may hold values from 0 to 1023
- nbr_coef: float32 [64, 4, 80, 1024], P('rows', 'cols'), may hold values from -0.625 to 0.625
- send_rows: int32 [64, 4, 4, 128], P('rows', 'cols'), may hold values from 0 to 511
Outputs:
- solution: float32 [32, 131072], P(None, ('rows', 'cols'))
- residual: float32 [32, 131072], P(None, ('rows', 'cols'))
The draws below stay inside these ranges and needn't reach their ends.
Inputs may be any that keep to these rules, and one draw needn't show every extreme that they name: `local_inverse`: each subdomain inverse has a diagonal between 0.25 and 2 and small off-diagonal entries. `coarse_inverse`: a diagonal between 0.25 and 2 at entries whose row and column name the same coarse unknown, small entries elsewhere.
All inputs are finite; a program needn't handle non-finite values.
Results may differ from the reference program's by a relative error of at most 0.00013.
Values sent between devices are 32-bit elements; how exact they have to be, the bound alone decides.
A program may use at most 128 MiB of HBM per device.

```python
import math
import jax
import jax.numpy as jnp
from jax import lax

NRHS = 32
SUB = 1024
OVB = 128
MODES = 64
COUPLINGS = 80
OWN = 512
DEV_ROWS = 64
DEV_COLS = 4
UNKNOWNS = 131072
COARSE = 16384


def draw_local_inverse(key, part):
    key_off, key_diag = jax.random.split(jax.random.fold_in(key, 11))
    shape = (DEV_ROWS, DEV_COLS, SUB, SUB)
    off = jnp.clip(jax.random.normal(key_off, shape, jnp.float32), -6.0, 6.0) * (0.5 / math.sqrt(SUB))
    diag_vals = jax.random.uniform(key_diag, (DEV_ROWS, DEV_COLS, SUB, 1), jnp.float32, 0.5, 1.5)
    row_ids = jnp.arange(SUB, dtype=jnp.int32)[:, None]
    col_ids = jnp.arange(SUB, dtype=jnp.int32)[None, :]
    unit = (row_ids == col_ids).astype(jnp.float32)
    return off + unit * diag_vals


def draw_coarse_inverse(key, part):
    key_off, key_diag = jax.random.split(jax.random.fold_in(key, 23))
    shape = (COARSE, COARSE)
    off = jnp.clip(jax.random.normal(key_off, shape, jnp.float32), -6.0, 6.0) * (0.5 / math.sqrt(COARSE))
    diag_vals = jax.random.uniform(key_diag, (COARSE, 1), jnp.float32, 0.5, 1.5)
    row_ids = jnp.arange(COARSE, dtype=jnp.int32)
    row_dev = row_ids // (DEV_COLS * MODES)
    col_dev = row_ids // MODES % DEV_COLS
    mode_id = row_ids % MODES
    target = (col_dev * DEV_ROWS + row_dev) * MODES + mode_id
    col_ids = jnp.arange(COARSE, dtype=jnp.int32)[None, :]
    unit = (col_ids == target[:, None]).astype(jnp.float32)
    return off + unit * diag_vals


def place_ends(drawn, key, smallest, largest):
    extent = drawn.shape
    spot = [jax.random.randint(jax.random.fold_in(key, axis), (), 0, extent[axis]) for axis in range(len(extent))]
    drawn = drawn.at[tuple(spot)].set(smallest)
    longest = extent.index(max(extent))
    spot[longest] = (spot[longest] + 1) % extent[longest]
    return drawn.at[tuple(spot)].set(largest)


def steps_of(own_key, extent, shards, low, top_value):
    def one(dim, blocks):
        steps = jax.random.uniform(jax.random.fold_in(jax.random.fold_in(own_key, 6), dim), (blocks,), jnp.float32, low / len(shards), top_value / len(shards))
        return jnp.repeat(jnp.exp(steps), extent[dim] // blocks).reshape((-1,) + (1,) * (len(extent) - dim - 1))

    loudness = one(*shards[0])
    for cut in shards[1:]:
        loudness = loudness * one(*cut)
    return loudness


def scatter_about(rng, dims, spread, reach, cuts=(), kind=jnp.bfloat16):
    gain = steps_of(rng, dims, cuts, -0.22, 0.18) if cuts else 1.0
    array = jax.random.normal(rng, dims, jnp.float32) * spread * gain
    return jnp.minimum(jnp.maximum(array, -reach), reach).astype(kind)


def setup_inputs(seed: int = 0) -> dict:
    key_list = jax.random.split(jax.random.key(seed), 9)
    right_side = scatter_about(key_list[0], (NRHS, UNKNOWNS), 1.0, 6.0, ((1, 256),), jnp.float32)
    local_inverse = draw_local_inverse(jax.random.fold_in(key_list[8], 71), 0)
    modes = scatter_about(key_list[2], (DEV_ROWS, DEV_COLS, MODES, SUB), SUB ** -0.5, 0.1875, ((0, 64), (1, 4)), jnp.float32)
    coarse_inverse = draw_coarse_inverse(jax.random.fold_in(key_list[8], 71), 0)
    stiff_diag = jnp.clip(jnp.exp(math.log(4.0) - 1.3862944 * jax.random.uniform(key_list[4], (DEV_ROWS, DEV_COLS, SUB), jnp.float32) ** steps_of(key_list[4], (DEV_ROWS, DEV_COLS, SUB), ((0, 64), (1, 4)), -0.2, 0.2)), 1.0, 4.0)
    nbr_index = place_ends(jax.random.randint(key_list[5], (DEV_ROWS, DEV_COLS, COUPLINGS, SUB), 0, SUB), jax.random.fold_in(key_list[5], 1), 0, SUB - 1).astype(jnp.int32)
    nbr_coef = scatter_about(key_list[6], (DEV_ROWS, DEV_COLS, COUPLINGS, SUB), COUPLINGS ** -0.5, 0.625, ((0, 64), (1, 4)), jnp.float32)
    send_rows = place_ends(jax.random.randint(key_list[7], (DEV_ROWS, DEV_COLS, 4, OVB), 0, OWN), jax.random.fold_in(key_list[7], 1), 0, OWN - 1).astype(jnp.int32)
    return dict(right_side=right_side, local_inverse=local_inverse, modes=modes, coarse_inverse=coarse_inverse, stiff_diag=stiff_diag, nbr_index=nbr_index, nbr_coef=nbr_coef, send_rows=send_rows)


def from_lower(field, axis):
    edge = jnp.zeros_like(lax.slice_in_dim(field, 0, 1, axis=axis))
    return jnp.concatenate([edge, lax.slice_in_dim(field, 0, field.shape[axis] - 1, axis=axis)], axis)


def from_upper(field, axis):
    edge = jnp.zeros_like(lax.slice_in_dim(field, 0, 1, axis=axis))
    return jnp.concatenate([lax.slice_in_dim(field, 1, field.shape[axis], axis=axis), edge], axis)


def pick_rows(owned, sends):
    return jnp.stack([owned[:, sends[e]] for e in range(4)], axis=0)


def extend(owned, sends):
    picked = jax.vmap(jax.vmap(pick_rows))(owned, sends)
    first = from_lower(picked[:, :, 0], 0)
    second = from_upper(picked[:, :, 1], 0)
    third = from_lower(picked[:, :, 2], 1)
    fourth = from_upper(picked[:, :, 3], 1)
    return jnp.concatenate([owned, first, second, third, fourth], axis=-1)


def place_rows(owned, sends, backs):
    for e in range(4):
        owned = owned.at[:, sends[e]].add(backs[e])
    return owned


def fold(sub, sends):
    owned = sub[..., :OWN]
    bands = [sub[..., OWN + e * OVB:OWN + (e + 1) * OVB] for e in range(4)]
    backs = jnp.stack([from_upper(bands[0], 0), from_lower(bands[1], 0), from_upper(bands[2], 1), from_lower(bands[3], 1)], axis=2)
    return jax.vmap(jax.vmap(place_rows))(owned, sends, backs)


def couple_one(sub, diag, index, coef):
    def step(total, pair):
        idx, weight = pair
        return total + weight[None, :] * sub[:, idx], None

    total, unused = lax.scan(step, diag[None, :] * sub, (index, coef))
    return total


def precondition(resid, local_inverse, modes, coarse_inverse, sends):
    sub = extend(resid, sends)
    hi = lax.Precision.HIGHEST
    local = jnp.einsum("rcns,rcts->rcnt", sub, local_inverse, precision=hi)
    restricted = jnp.einsum("rcns,rcms->rcnm", sub, modes, precision=hi)
    ordered = jnp.transpose(restricted, (2, 1, 0, 3)).reshape(NRHS, COARSE)
    product = lax.dot_general(ordered, coarse_inverse, (((1,), (1,)), ((), ())), precision=hi, preferred_element_type=jnp.float32)
    coarse = jnp.transpose(product.reshape(NRHS, DEV_ROWS, DEV_COLS, MODES), (1, 2, 0, 3))
    local = local + jnp.einsum("rcnm,rcms->rcns", coarse, modes, precision=hi)
    return fold(local, sends)


def reference(right_side, local_inverse, modes, coarse_inverse, stiff_diag, nbr_index, nbr_coef, send_rows):
    rhs = jnp.transpose(right_side.reshape(NRHS, DEV_ROWS, DEV_COLS, OWN), (1, 2, 0, 3))
    first = precondition(rhs, local_inverse, modes, coarse_inverse, send_rows)
    sub = extend(first, send_rows)
    image = fold(jax.vmap(jax.vmap(couple_one))(sub, stiff_diag, nbr_index, nbr_coef), send_rows)
    resid = rhs - image
    second = first + precondition(resid, local_inverse, modes, coarse_inverse, send_rows)
    solution = jnp.transpose(second, (2, 0, 1, 3)).reshape(NRHS, UNKNOWNS)
    residual = jnp.transpose(resid, (2, 0, 1, 3)).reshape(NRHS, UNKNOWNS)
    return solution, residual
```

```python
import jax
import jax.numpy as jnp
from jax import lax
from jax.experimental import pallas as pl
from jax.experimental.pallas import tpu as pltpu
from jax.sharding import PartitionSpec as P

BF = jnp.bfloat16
F32 = jnp.float32
NT = (((1,), (1,)), ((), ()))
NN = (((1,), (0,)), ((), ()))
UNROLL = 64


def dot(a, b, dims):
    return lax.dot_general(a, b, dims, preferred_element_type=F32)


def halves(x):
    hi = x.astype(BF)
    return hi, (x - hi.astype(F32)).astype(BF)


def split_into(src, high, low, rows, step):
    def part(t, carry):
        at = pl.ds(pl.multiple_of(t * step, step), step)
        hi, lo = halves(src[at, :])
        high[at, :] = hi
        low[at, :] = lo
        return carry

    lax.fori_loop(0, rows // step, part, 0)


def dot_twice(x, w, dims):
    n = x.shape[0]
    hi, lo = halves(x)
    both = dot(jnp.concatenate([hi, lo], 0), w, dims)
    return both[:n] + both[n:]


def dot_thrice(x, high, low, dims):
    n = x.shape[0]
    hi, lo = halves(x)
    both = dot(jnp.concatenate([hi, lo], 0), high, dims)
    return both[:n] + both[n:] + dot(hi, low, dims)


def kernel(
    rhs_ref, inv_hbm, modes_hbm, coarse_hbm, diag_ref, index_hbm, coef_hbm, sends_ref,
    sol_ref, res_ref,
    inv_raw, coarse_raw, modes_raw, index_raw, coef_raw,
    inv_hi, inv_lo, coarse_hi, coarse_lo, modes_hi, modes_lo,
    pick_mat, low_t, high_t, coef_hi, coef_lo, tiles, stiff_hi, stiff_lo,
    x_hi, halo_out, halo_in, gathered, parts, others, local_buf, first_buf,
    load_sem, halo_send, halo_recv, y_send, y_recv, z_send, z_recv, x_send, x_recv,
    col_send, col_recv,
):
    i = lax.axis_index("rows")
    j = lax.axis_index("cols")
    gx = i // 16
    gy = lax.rem(i // 8, 2)
    gz = lax.rem(i, 8)

    def row_of(x, y, z):
        return x * 16 + y * 8 + z

    loads = [
        pltpu.make_async_copy(s, d, load_sem.at[n])
        for n, (s, d) in enumerate(
            [
                (modes_hbm, modes_raw),
                (index_hbm, index_raw),
                (coef_hbm, coef_raw),
                (inv_hbm, inv_raw),
                (coarse_hbm, coarse_raw),
            ]
        )
    ]
    for load in loads:
        load.start()

    beside = [
        (lax.rem(i + 1, 64), j),
        (lax.rem(i + 63, 64), j),
        (i, lax.rem(j + 1, 4)),
        (i, lax.rem(j + 3, 4)),
    ]
    y_peer = (row_of(gx, 1 - gy, gz), j)

    def z_peer(d):
        return (row_of(gx, gy, lax.rem(gz + d, 8)), j)

    def x_peer(d):
        return (row_of(lax.rem(gx + d, 4), gy, gz), j)

    barrier = pltpu.get_barrier_semaphore()
    greet = beside + [(i, lax.rem(j + 2, 4)), y_peer]
    greet = greet + [z_peer(d) for d in range(1, 8)] + [x_peer(d) for d in range(1, 4)]
    for peer in greet:
        pl.semaphore_signal(barrier, inc=1, device_id=peer, device_id_type=pl.DeviceIdType.MESH)

    row_ids = lax.broadcasted_iota(jnp.int32, (512, 128), 0)
    for e in range(4):
        hit = row_ids == jnp.broadcast_to(sends_ref[e : e + 1, :], (512, 128))
        pick_mat[:, e * 128 : (e + 1) * 128] = jnp.where(hit, 1.0, 0.0).astype(BF)

    has = [i > 0, i < 63, j > 0, j < 3]

    def halo_copy(k, e, way):
        return pltpu.make_async_remote_copy(
            src_ref=halo_out.at[k, e],
            dst_ref=halo_in.at[k, e],
            send_sem=halo_send.at[k, e],
            recv_sem=halo_recv.at[k, e],
            device_id=beside[way],
            device_id_type=pl.DeviceIdType.MESH,
        )

    def halo_start(k, values, back):
        for e in range(4):
            halo_out[k, e] = values[:, e * 128 : (e + 1) * 128]
            halo_copy(k, e, e ^ back).start()

    def halo_wait(k, back):
        got = []
        for e in range(4):
            halo_copy(k, e, e ^ back).wait_recv()
            got.append(jnp.where(has[e ^ back], halo_in[k, e], 0.0))
        return jnp.concatenate(got, 1)

    lane = lax.broadcasted_iota(jnp.int32, (16, 128), 1)
    left = lane < 64

    def pair_at(x, z):
        return pl.ds(x * 16 + z * 2, 2)

    def remote(src, dst, send, recv, peer):
        return pltpu.make_async_remote_copy(
            src_ref=src,
            dst_ref=dst,
            send_sem=send,
            recv_sem=recv,
            device_id=peer,
            device_id_type=pl.DeviceIdType.MESH,
        )

    def y_copy(k, y):
        at = gathered.at[k, pl.ds(gx * 16 + gz * 2 + y, 1)]
        return remote(at, at, y_send.at[k], y_recv.at[k], y_peer)

    def z_copy(k, d, z):
        at = gathered.at[k, pair_at(gx, z)]
        return remote(at, at, z_send.at[k, d], z_recv.at[k, d], z_peer(d))

    def x_copy(k, d, dx, x):
        at = gathered.at[k, pair_at(x, lax.rem(gz - d + 8, 8))]
        return remote(at, at, x_send.at[k, d, dx], x_recv.at[k, d, dx], x_peer(dx))

    def col_copy(k, d, slot):
        return remote(
            parts.at[k, slot],
            others.at[k, d],
            col_send.at[k, d],
            col_recv.at[k, d],
            (i, lax.rem(j + d, 4)),
        )

    def gather_start(k, restricted):
        block = jnp.where(left, restricted[:16], restricted[16:])
        gathered[k, pl.ds(gx * 16 + gz * 2 + gy, 1)] = block.reshape(1, 16, 128)
        y_copy(k, gy).start()

    def gather_spread(k, work):
        y_copy(k, 1 - gy).wait_recv()
        for d in (1, 7, 2, 6, 3, 5, 4):
            z_copy(k, d, gz).start()
        for dx in (1, 3, 2):
            x_copy(k, 0, dx, gx).start()
        work(0)

        def step(t, carry):
            d = jnp.where(lax.rem(t, 2) == 1, (t + 1) // 2, 8 - t // 2)
            z_copy(k, d, lax.rem(gz - d + 8, 8)).wait_recv()
            for dx in (1, 3, 2):
                x_copy(k, d, dx, gx).start()
            work(t)
            return carry

        lax.fori_loop(1, 8, step, 0)

    def gather_finish(k):
        def step(d, carry):
            for dx in (1, 3, 2):
                x_copy(k, d, dx, lax.rem(gx - dx + 4, 4)).wait_recv()
            return carry

        lax.fori_loop(0, 8, step, 0)

    def coarse_apply(k):
        for x in range(4):
            for y in range(2):
                for zz in range(4):
                    a = gathered[k, x * 16 + zz * 4 + y]
                    b = gathered[k, x * 16 + zz * 4 + 2 + y]
                    top = jnp.where(left, a, pltpu.roll(b, 64, 1))
                    low = jnp.where(left, pltpu.roll(a, 64, 1), b)
                    hi, lo = halves(jnp.concatenate([top, low], 0))
                    at = pl.ds((x * 8 + y * 4 + zz) * 128, 128)
                    x_hi[0:32, at] = hi
                    x_hi[32:64, at] = lo
        both = dot(x_hi[...], coarse_hi[...], NT)
        part = both[:32] + both[32:] + dot(x_hi[0:32, :], coarse_lo[...], NT)
        for c in range(4):
            a = part[:16, (c // 2) * 128 : (c // 2) * 128 + 128]
            b = part[16:, (c // 2) * 128 : (c // 2) * 128 + 128]
            if c % 2 == 0:
                packed = jnp.where(left, a, pltpu.roll(b, 64, 1))
            else:
                packed = jnp.where(left, pltpu.roll(a, 64, 1), b)
            parts[k, c] = packed
        for d in (2, 1, 3):
            col_copy(k, d, lax.rem(j + d, 4)).start()

    def coarse_finish(k):
        total = parts[k, j]
        for d in (1, 3, 2):
            col_copy(k, d, lax.rem(j + d, 4)).wait_recv()
            total = total + others[k, d]
        zero = jnp.zeros_like(total)
        return jnp.concatenate([jnp.where(left, total, zero), jnp.where(left, zero, total)], 0)

    def restrict(own, cols):
        return dot_thrice(own, modes_hi[:, cols], modes_lo[:, cols], NT)

    own_cols = slice(0, 512)
    rim_cols = slice(512, 1024)

    def pick(field):
        return dot_twice(field, pick_mat[...], NN)

    def scatter(bands):
        return dot_twice(bands, pick_mat[...], NT)

    rhs = rhs_ref[...]
    picked = pick(rhs)
    pl.semaphore_wait(barrier, len(greet))
    halo_start(0, picked, 0)

    loads[0].wait()
    m_hi, m_lo = halves(modes_raw[...])
    modes_hi[...] = jnp.concatenate([m_hi, m_hi], 0)
    modes_lo[...] = jnp.concatenate([m_lo, m_lo], 0)

    def stiff_prepare():
        loads[1].wait()
        loads[2].wait()

        def turn(t, carry):
            at = pl.ds(pl.multiple_of(t * 128, 128), 128)
            idx = jnp.concatenate([index_raw[:, at], jnp.zeros((48, 128), jnp.int32)], 0).T
            val = jnp.concatenate([coef_raw[:, at], jnp.zeros((48, 128), F32)], 0).T
            low_t[at, :] = (idx & 127).astype(F32)
            high_t[at, :] = (idx >> 7).astype(F32)
            hi = val.astype(BF).astype(F32)
            coef_hi[at, :] = hi
            coef_lo[at, :] = val - hi
            return carry

        lax.fori_loop(0, 8, turn, 0)

    def stiff_build(t):
        lanes = lax.broadcasted_iota(jnp.int32, (128, 128), 0).astype(F32).astype(BF)
        blocks = lax.broadcasted_iota(jnp.int32, (8, 128), 0).astype(F32)
        one = jnp.ones((128, 128), BF)
        none = jnp.zeros((128, 128), BF)
        blank = jnp.zeros((16, 128), BF)

        def some(g, carry):
            for q in range(UNROLL // 4):
                hot = []
                val = []
                s = t * 128 + g * UNROLL + q * 4
                for r in range(4):
                    at = pl.ds(s + r, 1)
                    low = jnp.broadcast_to(low_t[at, :], (128, 128)).astype(BF)
                    hot.append(jnp.where(low == lanes, one, none))
                    hit = jnp.broadcast_to(high_t[at, :], (8, 128)) == blocks
                    pair = [jnp.where(hit, coef_hi[at, :], 0.0), jnp.where(hit, coef_lo[at, :], 0.0)]
                    val.append(jnp.concatenate(pair, 0).astype(BF))
                right = jnp.concatenate(
                    [jnp.concatenate(hot[:2], 1), jnp.concatenate(hot[2:], 1)], 0
                )
                rows = [
                    jnp.concatenate([val[r], blank] if r % 2 == 0 else [blank, val[r]], 1)
                    for r in range(4)
                ]
                out = dot(jnp.concatenate(rows, 0), right, NT)
                for r in range(4):
                    cut = out[16 * r : 16 * r + 16, (r // 2) * 128 : (r // 2) * 128 + 128]
                    tiles[pl.ds(pl.multiple_of((s + r) * 8, 8), 8), :] = cut[:8] + cut[8:]
            return carry

        lax.fori_loop(0, 128 // UNROLL, some, 0)

    def stiff_finish():
        for r in range(4):
            for c in range(8):
                hi, lo = halves(tiles[pl.ds(c + r * 2048, 256, stride=8), :])
                stiff_hi[r * 256 : r * 256 + 256, c * 128 : c * 128 + 128] = hi
                stiff_lo[r * 256 : r * 256 + 256, c * 128 : c * 128 + 128] = lo

    def precondition(k, resid, ext_k, fold_k, prepare, work, late):
        restricted = restrict(resid, own_cols)
        prepare()
        rim = halo_wait(ext_k, 0)
        gather_start(k, restricted + restrict(rim, rim_cols))
        gather_spread(k, work)
        late()
        local_buf[...] = dot_thrice(
            jnp.concatenate([resid, rim], 1), inv_hi[...], inv_lo[...], NT
        )
        gather_finish(k)
        coarse_apply(k)
        if k == 0:
            stiff_finish()
        spread = coarse_finish(k)
        bands = local_buf[:, rim_cols] + dot_thrice(
            spread, modes_hi[:, rim_cols], modes_lo[:, rim_cols], NN
        )
        halo_start(fold_k, bands, 1)
        own = local_buf[:, own_cols] + dot_thrice(
            spread, modes_hi[:, own_cols], modes_lo[:, own_cols], NN
        )
        return own + scatter(halo_wait(fold_k, 1))

    def late_first():
        loads[3].wait()
        split_into(inv_raw, inv_hi, inv_lo, 1024, 128)
        loads[4].wait()
        split_into(coarse_raw, coarse_hi, coarse_lo, 256, 32)

    first = precondition(0, rhs, 0, 1, stiff_prepare, stiff_build, late_first)
    halo_start(2, pick(first), 0)
    first_buf[...] = first
    part = dot_thrice(first, stiff_hi[:, own_cols], stiff_lo[:, own_cols], NT)
    rim = halo_wait(2, 0)
    diag = diag_ref[...]
    bands = part[:, rim_cols] + diag[:, rim_cols] * rim + dot_thrice(
        rim, stiff_hi[rim_cols, rim_cols], stiff_lo[rim_cols, rim_cols], NT
    )
    halo_start(3, bands, 1)
    own = part[:, own_cols] + diag[:, own_cols] * first + dot_thrice(
        rim, stiff_hi[own_cols, rim_cols], stiff_lo[own_cols, rim_cols], NT
    )
    residual = rhs - (own + scatter(halo_wait(3, 1)))
    halo_start(4, pick(residual), 0)
    res_ref[...] = residual

    def nothing(*unused):
        return None

    second = precondition(1, residual, 4, 5, nothing, nothing, nothing)
    sol_ref[...] = first_buf[...] + second

    for k in range(6):
        for e in range(4):
            halo_copy(k, e, e ^ (k % 2)).wait_send()
    for k in range(2):
        y_copy(k, gy).wait_send()
        for d in range(1, 4):
            col_copy(k, d, lax.rem(j + d, 4)).wait_send()

        def drain_z(d, carry, k=k):
            z_copy(k, d, gz).wait_send()
            return carry

        def drain_x(d, carry, k=k):
            for dx in range(1, 4):
                x_copy(k, d, dx, gx).wait_send()
            return carry

        lax.fori_loop(1, 8, drain_z, 0)
        lax.fori_loop(0, 8, drain_x, 0)


def body(
    right_side, local_inverse, modes, coarse_inverse, stiff_diag, nbr_index, nbr_coef, send_rows
):
    vmem = pl.BlockSpec(memory_space=pltpu.VMEM)
    hbm = pl.BlockSpec(memory_space=pl.ANY)
    field = jax.ShapeDtypeStruct((32, 512), F32)
    dma = pltpu.SemaphoreType.DMA
    scratch = [
        pltpu.VMEM((1024, 1024), F32),
        pltpu.VMEM((256, 4096), F32),
        pltpu.VMEM((64, 1024), F32),
        pltpu.VMEM((80, 1024), jnp.int32),
        pltpu.VMEM((80, 1024), F32),
        pltpu.VMEM((1024, 1024), BF),
        pltpu.VMEM((1024, 1024), BF),
        pltpu.VMEM((256, 4096), BF),
        pltpu.VMEM((256, 4096), BF),
        pltpu.VMEM((128, 1024), BF),
        pltpu.VMEM((128, 1024), BF),
        pltpu.VMEM((512, 512), BF),
        pltpu.VMEM((1024, 128), F32),
        pltpu.VMEM((1024, 128), F32),
        pltpu.VMEM((1024, 128), F32),
        pltpu.VMEM((1024, 128), F32),
        pltpu.VMEM((8192, 128), F32),
        pltpu.VMEM((1024, 1024), BF),
        pltpu.VMEM((1024, 1024), BF),
        pltpu.VMEM((64, 4096), BF),
        pltpu.VMEM((6, 4, 32, 128), F32),
        pltpu.VMEM((6, 4, 32, 128), F32),
        pltpu.VMEM((2, 64, 16, 128), F32),
        pltpu.VMEM((2, 4, 16, 128), F32),
        pltpu.VMEM((2, 4, 16, 128), F32),
        pltpu.VMEM((32, 1024), F32),
        pltpu.VMEM((32, 512), F32),
        dma((5,)),
        dma((6, 4)),
        dma((6, 4)),
        dma((2,)),
        dma((2,)),
        dma((2, 8)),
        dma((2, 8)),
        dma((2, 8, 4)),
        dma((2, 8, 4)),
        dma((2, 4)),
        dma((2, 4)),
    ]
    return tuple(
        pl.pallas_call(
            kernel,
            out_shape=(field, field),
            in_specs=[vmem, hbm, hbm, hbm, vmem, hbm, hbm, vmem],
            out_specs=(vmem, vmem),
            scratch_shapes=scratch,
            compiler_params=pltpu.CompilerParams(
                collective_id=0, has_side_effects=True, vmem_limit_bytes=48 * 2**20
            ),
            name="schwarz",
        )(
            right_side,
            local_inverse[0, 0],
            modes[0, 0],
            coarse_inverse,
            stiff_diag[0],
            nbr_index[0, 0],
            nbr_coef[0, 0],
            send_rows[0, 0],
        )
    )


def solution(mesh):
    in_specs = (
        P(None, ("rows", "cols")),
        P("rows", "cols", None, None),
        P("rows", "cols", None, None),
        P("rows", "cols"),
        P("rows", "cols", None),
        P("rows", "cols", None, None),
        P("rows", "cols", None, None),
        P("rows", "cols", None, None),
    )
    out_specs = (P(None, ("rows", "cols")), P(None, ("rows", "cols")))
    return jax.shard_map(body, mesh=mesh, in_specs=in_specs, out_specs=out_specs, check_vma=False)
```

```python
import jax
import jax.numpy as jnp
from jax import lax
from jax.experimental import pallas as pl
from jax.experimental.pallas import tpu as pltpu
from jax.sharding import PartitionSpec as P

BF = jnp.bfloat16
F32 = jnp.float32
NT = (((1,), (1,)), ((), ()))
NN = (((1,), (0,)), ((), ()))
UNROLL = 64


def dot(a, b, dims):
    return lax.dot_general(a, b, dims, preferred_element_type=F32)


def halves(x):
    hi = x.astype(BF)
    return hi, (x - hi.astype(F32)).astype(BF)


def split_into(src, high, low, rows, step):
    def part(t, carry):
        at = pl.ds(pl.multiple_of(t * step, step), step)
        hi, lo = halves(src[at, :])
        high[at, :] = hi
        low[at, :] = lo
        return carry

    lax.fori_loop(0, rows // step, part, 0)


def dot_twice(x, w, dims):
    n = x.shape[0]
    hi, lo = halves(x)
    both = dot(jnp.concatenate([hi, lo], 0), w, dims)
    return both[:n] + both[n:]


def dot_thrice(x, high, low, dims):
    n = x.shape[0]
    hi, lo = halves(x)
    both = dot(jnp.concatenate([hi, lo], 0), high, dims)
    return both[:n] + both[n:] + dot(hi, low, dims)


def kernel(
    rhs_hbm, inv_hbm, modes_hbm, coarse_hbm, diag_hbm, index_hbm, coef_hbm, sends_hbm,
    sol_hbm, res_hbm,
    rhs_ref, diag_ref, sends_ref, inv_raw, coarse_raw, modes_raw, index_raw, coef_raw,
    inv_hi, inv_lo, coarse_hi, coarse_lo, modes_hi, modes_lo,
    pick_mat, pick_t, gram, res_buf, low_t, high_t, coef_hi, coef_lo, tiles, stiff_hi, stiff_lo,
    x_hi, halo_out, halo_in, gathered, parts, others, local_buf, first_buf,
    load_sem, halo_send, halo_recv, plane_send, plane_recv, x_send, x_recv,
    col_send, col_recv,
):
    i = lax.axis_index("rows")
    j = lax.axis_index("cols")
    gx = i // 16
    gy = lax.rem(i // 8, 2)
    gz = lax.rem(i, 8)

    def row_of(x, y, z):
        return x * 16 + y * 8 + z

    loads = [
        pltpu.make_async_copy(s, d, load_sem.at[n])
        for n, (s, d) in enumerate(
            [
                (sends_hbm, sends_ref),
                (rhs_hbm, rhs_ref),
                (modes_hbm, modes_raw),
                (diag_hbm, diag_ref),
                (index_hbm, index_raw),
                (coef_hbm, coef_raw),
                (inv_hbm, inv_raw),
                (coarse_hbm, coarse_raw),
            ]
        )
    ]
    for load in loads:
        load.start()

    beside = [
        (lax.rem(i + 1, 64), j),
        (lax.rem(i + 63, 64), j),
        (i, lax.rem(j + 1, 4)),
        (i, lax.rem(j + 3, 4)),
    ]

    def plane_peer(flip, d):
        return (row_of(gx, 1 - gy if flip else gy, lax.rem(gz + d, 8)), j)

    def x_peer(d):
        return (row_of(lax.rem(gx + d, 4), gy, gz), j)

    unsent = []
    barrier = pltpu.get_barrier_semaphore()
    greet = [plane_peer(flip, d) for d in (4, 3, 5, 2, 6, 1, 7, 0) for flip in (1, 0) if flip or d]
    greet = greet + [x_peer(d) for d in (2, 1, 3)] + beside + [(i, lax.rem(j + 2, 4))]
    for peer in greet:
        pl.semaphore_signal(barrier, inc=1, device_id=peer, device_id_type=pl.DeviceIdType.MESH)

    loads[0].wait()
    row_ids = lax.broadcasted_iota(jnp.int32, (512, 128), 0)
    for e in range(4):
        hit = row_ids == jnp.broadcast_to(sends_ref[e : e + 1, :], (512, 128))
        pick_mat[:, e * 128 : (e + 1) * 128] = jnp.where(hit, 1.0, 0.0).astype(BF)

    has = [i > 0, i < 63, j > 0, j < 3]

    def halo_copy(k, e, way):
        return pltpu.make_async_remote_copy(
            src_ref=halo_out.at[k, e],
            dst_ref=halo_in.at[k, e],
            send_sem=halo_send.at[k, e],
            recv_sem=halo_recv.at[k, e],
            device_id=beside[way],
            device_id_type=pl.DeviceIdType.MESH,
        )

    def halo_stage(k, values):
        for e in range(4):
            halo_out[k, e] = values[:, e * 128 : (e + 1) * 128]

    def halo_send_all(k, back):
        for e in range(4):
            halo_copy(k, e, e ^ back).start()
            unsent.append(lambda e=e: halo_copy(k, e, e ^ back).wait_send())

    def halo_start(k, values, back):
        halo_stage(k, values)
        halo_send_all(k, back)

    def halo_wait(k, back):
        got = []
        for e in range(4):
            halo_copy(k, e, e ^ back).wait_recv()
            got.append(jnp.where(has[e ^ back], halo_in[k, e], 0.0))
        return jnp.concatenate(got, 1)

    lane = lax.broadcasted_iota(jnp.int32, (16, 128), 1)
    left = lane < 64

    def pair_at(x, z):
        return pl.ds(x * 16 + z * 2, 2)

    def remote(src, dst, send, recv, peer):
        return pltpu.make_async_remote_copy(
            src_ref=src,
            dst_ref=dst,
            send_sem=send,
            recv_sem=recv,
            device_id=peer,
            device_id_type=pl.DeviceIdType.MESH,
        )

    def slot_at(y, z):
        return gx * 16 + z * 2 + y

    def plane_copy(k, flip, d, slot):
        at = gathered.at[k, pl.ds(slot, 1)]
        return remote(
            at, at, plane_send.at[k, flip, d], plane_recv.at[k, flip, d], plane_peer(flip, d)
        )

    def x_copy(k, d, dx, x):
        at = gathered.at[k, pair_at(x, lax.rem(gz - d + 8, 8))]
        return remote(at, at, x_send.at[k, d, dx], x_recv.at[k, d, dx], x_peer(dx))

    def col_copy(k, d, slot):
        return remote(
            parts.at[k, slot],
            others.at[k, d],
            col_send.at[k, d],
            col_recv.at[k, d],
            (i, lax.rem(j + d, 4)),
        )

    def gather_start(k, restricted):
        mine = slot_at(gy, gz)
        block = jnp.where(left, restricted[:16], restricted[16:])
        gathered[k, pl.ds(mine, 1)] = block.reshape(1, 16, 128)
        for d in (4, 3, 5, 2, 6, 1, 7, 0):
            for flip in (1, 0):
                if flip or d:
                    plane_copy(k, flip, d, mine).start()

        def drain(d, carry):
            plane_copy(k, 0, d, mine).wait_send()
            plane_copy(k, 1, d, mine).wait_send()
            return carry

        unsent.append(lambda: lax.fori_loop(1, 8, drain, 0))
        unsent.append(lambda: plane_copy(k, 1, 0, mine).wait_send())

    def gather_spread(k, work):
        plane_copy(k, 1, 0, slot_at(1 - gy, gz)).wait_recv()
        for dx in (2, 1, 3):
            x_copy(k, 0, dx, gx).start()

        def step(t, carry):
            d = jnp.where(lax.rem(t, 2) == 1, (t + 1) // 2, 8 - t // 2)
            z = lax.rem(gz - d + 8, 8)
            plane_copy(k, 0, d, slot_at(gy, z)).wait_recv()
            plane_copy(k, 1, d, slot_at(1 - gy, z)).wait_recv()
            for dx in (2, 1, 3):
                x_copy(k, d, dx, gx).start()
            work(t)
            return carry

        lax.fori_loop(1, 8, step, 0)

        def drain(d, carry):
            for dx in range(1, 4):
                x_copy(k, d, dx, gx).wait_send()
            return carry

        unsent.append(lambda: lax.fori_loop(0, 8, drain, 0))

    def coarse_group(k, x):
        for y in range(2):
            for zz in range(4):
                a = gathered[k, x * 16 + zz * 4 + y]
                b = gathered[k, x * 16 + zz * 4 + 2 + y]
                top = jnp.where(left, a, pltpu.roll(b, 64, 1))
                low = jnp.where(left, pltpu.roll(a, 64, 1), b)
                hi, lo = halves(jnp.concatenate([top, low], 0))
                at = pl.ds((y * 4 + zz) * 128, 128)
                x_hi[0:32, at] = hi
                x_hi[32:64, at] = lo
        at = pl.ds(pl.multiple_of(x * 1024, 1024), 1024)
        both = dot(x_hi[...], coarse_hi[:, at], NT)
        return both[:32] + both[32:] + dot(x_hi[0:32, :], coarse_lo[:, at], NT)

    def coarse_apply(k):
        part = coarse_group(k, gx)
        for dx in (1, 3, 2):
            x = lax.rem(gx - dx + 4, 4)

            def arrived(d, carry, dx=dx, x=x):
                x_copy(k, d, dx, x).wait_recv()
                return carry

            lax.fori_loop(0, 8, arrived, 0)
            part = part + coarse_group(k, x)
        for c in range(4):
            a = part[:16, (c // 2) * 128 : (c // 2) * 128 + 128]
            b = part[16:, (c // 2) * 128 : (c // 2) * 128 + 128]
            if c % 2 == 0:
                packed = jnp.where(left, a, pltpu.roll(b, 64, 1))
            else:
                packed = jnp.where(left, pltpu.roll(a, 64, 1), b)
            parts[k, c] = packed
        for d in (2, 1, 3):
            col_copy(k, d, lax.rem(j + d, 4)).start()
            unsent.append(lambda d=d: col_copy(k, d, lax.rem(j + d, 4)).wait_send())

    def coarse_finish(k):
        total = parts[k, j]
        for d in (1, 3, 2):
            col_copy(k, d, lax.rem(j + d, 4)).wait_recv()
            total = total + others[k, d]
        zero = jnp.zeros_like(total)
        return jnp.concatenate([jnp.where(left, total, zero), jnp.where(left, zero, total)], 0)

    def restrict(own, cols):
        return dot_thrice(own, modes_hi[:, cols], modes_lo[:, cols], NT)

    own_cols = slice(0, 512)
    rim_cols = slice(512, 1024)

    def pick(field):
        return dot_twice(field, pick_mat[...], NN)

    def scatter(bands):
        return dot_twice(bands, pick_t[...], NN)

    def stiff_prepare():
        loads[4].wait()
        loads[5].wait()

        def turn(t, carry):
            at = pl.ds(pl.multiple_of(t * 128, 128), 128)
            idx = jnp.concatenate([index_raw[:, at], jnp.zeros((48, 128), jnp.int32)], 0).T
            val = jnp.concatenate([coef_raw[:, at], jnp.zeros((48, 128), F32)], 0).T
            low_t[at, :] = (idx & 127).astype(F32)
            high_t[at, :] = (idx >> 7).astype(F32)
            hi = val.astype(BF).astype(F32)
            coef_hi[at, :] = hi
            coef_lo[at, :] = val - hi
            return carry

        lax.fori_loop(0, 8, turn, 0)

    def stiff_build(begin, end):
        lanes = lax.broadcasted_iota(jnp.int32, (128, 128), 0).astype(F32).astype(BF)
        blocks = lax.broadcasted_iota(jnp.int32, (8, 128), 0).astype(F32)
        one = jnp.ones((128, 128), BF)
        none = jnp.zeros((128, 128), BF)
        blank = jnp.zeros((16, 128), BF)

        def some(g, carry):
            for q in range(UNROLL // 4):
                hot = []
                val = []
                s = g * UNROLL + q * 4
                for r in range(4):
                    at = pl.ds(s + r, 1)
                    low = jnp.broadcast_to(low_t[at, :], (128, 128)).astype(BF)
                    hot.append(jnp.where(low == lanes, one, none))
                    hit = jnp.broadcast_to(high_t[at, :], (8, 128)) == blocks
                    pair = [jnp.where(hit, coef_hi[at, :], 0.0), jnp.where(hit, coef_lo[at, :], 0.0)]
                    val.append(jnp.concatenate(pair, 0).astype(BF))
                right = jnp.concatenate(
                    [jnp.concatenate(hot[:2], 1), jnp.concatenate(hot[2:], 1)], 0
                )
                rows = [
                    jnp.concatenate([val[r], blank] if r % 2 == 0 else [blank, val[r]], 1)
                    for r in range(4)
                ]
                out = dot(jnp.concatenate(rows, 0), right, NT)
                for r in range(4):
                    cut = out[16 * r : 16 * r + 16, (r // 2) * 128 : (r // 2) * 128 + 128]
                    tiles[pl.ds(pl.multiple_of((s + r) * 8, 8), 8), :] = cut[:8] + cut[8:]
            return carry

        if begin is end:
            some(begin, 0)
        else:
            lax.fori_loop(begin, end, some, 0)

    def stiff_finish():
        for r in range(4):
            for c in range(8):
                hi, lo = halves(tiles[pl.ds(c + r * 2048, 256, stride=8), :])
                stiff_hi[r * 256 : r * 256 + 256, c * 128 : c * 128 + 128] = hi
                stiff_lo[r * 256 : r * 256 + 256, c * 128 : c * 128 + 128] = lo

    def local_solve(resid, rim):
        local_buf[...] = dot_thrice(jnp.concatenate([resid, rim], 1), inv_hi[...], inv_lo[...], NT)

    def spread_cols(spread, cols):
        return local_buf[:, cols] + dot_thrice(spread, modes_hi[:, cols], modes_lo[:, cols], NN)

    def start_fold(k, fold_k, spread):
        halo_start(fold_k, spread_cols(spread, rim_cols), 1)
        return spread_cols(spread, own_cols)

    def nothing(*unused):
        return None

    loads[1].wait()
    rhs = rhs_ref[...]
    halo_stage(0, pick(rhs))
    stiff_prepare()
    stiff_build(0, 4)
    pl.semaphore_wait(barrier, len(greet))
    halo_send_all(0, 0)

    loads[2].wait()
    m_hi, m_lo = halves(modes_raw[...])
    modes_hi[...] = jnp.concatenate([m_hi, m_hi], 0)
    modes_lo[...] = jnp.concatenate([m_lo, m_lo], 0)
    pick_t[...] = pick_mat[...].astype(F32).T.astype(BF)
    gram[...] = dot(pick_t[...], pick_mat[...], NN).astype(BF)
    stiff_build(4, 9)
    restricted = restrict(rhs, own_cols)
    rim = halo_wait(0, 0)
    def stiff_step(t):
        at = 8 + t
        stiff_build(at, at)

    gather_start(0, restricted + restrict(rim, rim_cols))
    loads[6].wait()
    split_into(inv_raw, inv_hi, inv_lo, 1024, 128)
    local_solve(rhs, rim)
    gather_spread(0, stiff_step)
    loads[7].wait()
    split_into(coarse_raw, coarse_hi, coarse_lo, 256, 32)
    coarse_apply(0)
    stiff_finish()
    spread = coarse_finish(0)
    own = start_fold(0, 1, spread)
    picked = pick(own)
    back = halo_wait(1, 1)
    halo_start(2, picked + dot_twice(back, gram[...], NN), 0)
    first = own + scatter(back)
    first_buf[...] = first

    part = dot_thrice(first, stiff_hi[:, own_cols], stiff_lo[:, own_cols], NT)
    loads[3].wait()
    diag = diag_ref[...]
    rim = halo_wait(2, 0)
    bands = part[:, rim_cols] + diag[:, rim_cols] * rim + dot_thrice(
        rim, stiff_hi[rim_cols, rim_cols], stiff_lo[rim_cols, rim_cols], NT
    )
    halo_start(3, bands, 1)
    own = part[:, own_cols] + diag[:, own_cols] * first + dot_thrice(
        rim, stiff_hi[own_cols, rim_cols], stiff_lo[own_cols, rim_cols], NT
    )
    own = rhs - own
    picked = pick(own)
    back = halo_wait(3, 1)
    halo_start(4, picked - dot_twice(back, gram[...], NN), 0)
    residual = own - scatter(back)
    res_buf[...] = residual
    res_copy = pltpu.make_async_copy(res_buf, res_hbm, load_sem.at[8])
    res_copy.start()

    restricted = restrict(residual, own_cols)
    rim = halo_wait(4, 0)
    gather_start(1, restricted + restrict(rim, rim_cols))
    local_solve(residual, rim)
    gather_spread(1, nothing)
    coarse_apply(1)
    spread = coarse_finish(1)
    own = first_buf[...] + start_fold(1, 5, spread)
    back = halo_wait(5, 1)
    first_buf[...] = own + scatter(back)
    sol_copy = pltpu.make_async_copy(first_buf, sol_hbm, load_sem.at[9])
    sol_copy.start()
    for finish in unsent:
        finish()
    res_copy.wait()
    sol_copy.wait()


def body(
    right_side, local_inverse, modes, coarse_inverse, stiff_diag, nbr_index, nbr_coef, send_rows
):
    hbm = pl.BlockSpec(memory_space=pltpu.HBM)
    field = jax.ShapeDtypeStruct((32, 512), F32)
    dma = pltpu.SemaphoreType.DMA
    scratch = [
        pltpu.VMEM((32, 512), F32),
        pltpu.VMEM((1, 1024), F32),
        pltpu.VMEM((4, 128), jnp.int32),
        pltpu.VMEM((1024, 1024), F32),
        pltpu.VMEM((256, 4096), F32),
        pltpu.VMEM((64, 1024), F32),
        pltpu.VMEM((80, 1024), jnp.int32),
        pltpu.VMEM((80, 1024), F32),
        pltpu.VMEM((1024, 1024), BF),
        pltpu.VMEM((1024, 1024), BF),
        pltpu.VMEM((256, 4096), BF),
        pltpu.VMEM((256, 4096), BF),
        pltpu.VMEM((128, 1024), BF),
        pltpu.VMEM((128, 1024), BF),
        pltpu.VMEM((512, 512), BF),
        pltpu.VMEM((512, 512), BF),
        pltpu.VMEM((512, 512), BF),
        pltpu.VMEM((32, 512), F32),
        pltpu.VMEM((1024, 128), F32),
        pltpu.VMEM((1024, 128), F32),
        pltpu.VMEM((1024, 128), F32),
        pltpu.VMEM((1024, 128), F32),
        pltpu.VMEM((8192, 128), F32),
        pltpu.VMEM((1024, 1024), BF),
        pltpu.VMEM((1024, 1024), BF),
        pltpu.VMEM((64, 1024), BF),
        pltpu.VMEM((6, 4, 32, 128), F32),
        pltpu.VMEM((6, 4, 32, 128), F32),
        pltpu.VMEM((2, 64, 16, 128), F32),
        pltpu.VMEM((2, 4, 16, 128), F32),
        pltpu.VMEM((2, 4, 16, 128), F32),
        pltpu.VMEM((32, 1024), F32),
        pltpu.VMEM((32, 512), F32),
        dma((10,)),
        dma((6, 4)),
        dma((6, 4)),
        dma((2, 2, 8)),
        dma((2, 2, 8)),
        dma((2, 8, 4)),
        dma((2, 8, 4)),
        dma((2, 4)),
        dma((2, 4)),
    ]
    return tuple(
        pl.pallas_call(
            kernel,
            out_shape=(field, field),
            in_specs=[hbm] * 8,
            out_specs=(hbm, hbm),
            scratch_shapes=scratch,
            compiler_params=pltpu.CompilerParams(
                collective_id=0, has_side_effects=True, vmem_limit_bytes=60 * 2**20
            ),
            name="schwarz",
        )(
            right_side,
            local_inverse[0, 0],
            modes[0, 0],
            coarse_inverse,
            stiff_diag[0],
            nbr_index[0, 0],
            nbr_coef[0, 0],
            send_rows[0, 0],
        )
    )


def solution(mesh):
    in_specs = (
        P(None, ("rows", "cols")),
        P("rows", "cols", None, None),
        P("rows", "cols", None, None),
        P("rows", "cols"),
        P("rows", "cols", None),
        P("rows", "cols", None, None),
        P("rows", "cols", None, None),
        P("rows", "cols", None, None),
    )
    out_specs = (P(None, ("rows", "cols")), P(None, ("rows", "cols")))
    return jax.shard_map(body, mesh=mesh, in_specs=in_specs, out_specs=out_specs, check_vma=False)
```

```python
import jax
import jax.numpy as jnp
from jax import lax
from jax.experimental import pallas as pl
from jax.experimental.pallas import tpu as pltpu
from jax.sharding import PartitionSpec as P

BF = jnp.bfloat16
F32 = jnp.float32
NT = (((1,), (1,)), ((), ()))
NN = (((1,), (0,)), ((), ()))
UNROLL = 64


def dot(a, b, dims):
    return lax.dot_general(a, b, dims, preferred_element_type=F32)


def halves(x):
    hi = x.astype(BF)
    return hi, (x - hi.astype(F32)).astype(BF)


def split_into(src, high, low, rows, step):
    def part(t, carry):
        at = pl.ds(pl.multiple_of(t * step, step), step)
        hi, lo = halves(src[at, :])
        high[at, :] = hi
        low[at, :] = lo
        return carry

    lax.fori_loop(0, rows // step, part, 0)


def dot_twice(x, w, dims):
    n = x.shape[0]
    hi, lo = halves(x)
    both = dot(jnp.concatenate([hi, lo], 0), w, dims)
    return both[:n] + both[n:]


def dot_thrice(x, high, low, dims):
    n = x.shape[0]
    hi, lo = halves(x)
    both = dot(jnp.concatenate([hi, lo], 0), high, dims)
    return both[:n] + both[n:] + dot(hi, low, dims)


def kernel(
    rhs_hbm, inv_hbm, modes_hbm, coarse_hbm, diag_hbm, index_hbm, coef_hbm, sends_hbm,
    sol_hbm, res_hbm,
    rhs_ref, diag_ref, sends_ref, inv_raw, coarse_raw, modes_raw, index_raw, coef_raw,
    inv_hi, inv_lo, coarse_hi, coarse_lo, modes_hi, modes_lo,
    pick_mat, pick_t, gram, res_buf, low_t, high_t, coef_hi, coef_lo, tiles, stiff_hi, stiff_lo,
    x_hi, own_buf, lent_buf, folded_hi, folded_lo, lent_hi, lent_lo, basis_in, near, halo_out, halo_in, gathered, parts, others, local_buf, first_buf,
    load_sem, halo_send, halo_recv, plane_send, plane_recv, x_send, x_recv,
    col_send, col_recv, row_send, row_recv, basis_send, basis_recv,
):
    i = lax.axis_index("rows")
    j = lax.axis_index("cols")
    gx = i // 16
    gy = lax.rem(i // 8, 2)
    gz = lax.rem(i, 8)

    def row_of(x, y, z):
        return x * 16 + y * 8 + z

    loads = [
        pltpu.make_async_copy(s, d, load_sem.at[n])
        for n, (s, d) in enumerate(
            [
                (sends_hbm, sends_ref),
                (rhs_hbm, rhs_ref),
                (modes_hbm, modes_raw),
                (diag_hbm, diag_ref),
                (index_hbm, index_raw),
                (coef_hbm, coef_raw),
                (inv_hbm, inv_raw),
                (coarse_hbm, coarse_raw),
            ]
        )
    ]
    for load in loads:
        load.start()

    beside = [
        (lax.rem(i + 1, 64), j),
        (lax.rem(i + 63, 64), j),
        (i, lax.rem(j + 1, 4)),
        (i, lax.rem(j + 3, 4)),
    ]

    def plane_peer(flip, d):
        return (row_of(gx, 1 - gy if flip else gy, lax.rem(gz + d, 8)), j)

    def x_peer(d):
        return (row_of(lax.rem(gx + d, 4), gy, gz), j)

    unsent = []
    barrier = pltpu.get_barrier_semaphore()
    greet = [plane_peer(flip, d) for d in (4, 3, 5, 2, 6, 1, 7, 0) for flip in (1, 0) if flip or d]
    greet = greet + [x_peer(d) for d in (2, 1, 3)] + [(i, lax.rem(j + d, 4)) for d in (2, 1, 3)]
    greet = greet + [(lax.rem(i + way, 64), lax.rem(j + d, 4)) for way in (1, 63) for d in range(4)]
    for peer in greet:
        pl.semaphore_signal(barrier, inc=1, device_id=peer, device_id_type=pl.DeviceIdType.MESH)

    loads[0].wait()
    row_ids = lax.broadcasted_iota(jnp.int32, (512, 128), 0)
    for e in range(4):
        hit = row_ids == jnp.broadcast_to(sends_ref[e : e + 1, :], (512, 128))
        pick_mat[:, e * 128 : (e + 1) * 128] = jnp.where(hit, 1.0, 0.0).astype(BF)

    has = [i > 0, i < 63, j > 0, j < 3]

    def halo_copy(k, e, way):
        return pltpu.make_async_remote_copy(
            src_ref=halo_out.at[k, e],
            dst_ref=halo_in.at[k, e],
            send_sem=halo_send.at[k, e],
            recv_sem=halo_recv.at[k, e],
            device_id=beside[way],
            device_id_type=pl.DeviceIdType.MESH,
        )

    def halo_stage(k, values):
        for e in range(4):
            halo_out[k, e] = values[:, e * 128 : (e + 1) * 128]

    def halo_send_all(k, back):
        for e in range(4):
            halo_copy(k, e, e ^ back).start()
            unsent.append(lambda e=e: halo_copy(k, e, e ^ back).wait_send())

    def halo_start(k, values, back):
        halo_stage(k, values)
        halo_send_all(k, back)

    def halo_wait(k, back):
        got = []
        for e in range(4):
            halo_copy(k, e, e ^ back).wait_recv()
            got.append(jnp.where(has[e ^ back], halo_in[k, e], 0.0))
        return jnp.concatenate(got, 1)

    lane = lax.broadcasted_iota(jnp.int32, (16, 128), 1)
    left = lane < 64

    def pair_at(x, z):
        return pl.ds(x * 16 + z * 2, 2)

    def remote(src, dst, send, recv, peer):
        return pltpu.make_async_remote_copy(
            src_ref=src,
            dst_ref=dst,
            send_sem=send,
            recv_sem=recv,
            device_id=peer,
            device_id_type=pl.DeviceIdType.MESH,
        )

    def slot_at(y, z):
        return gx * 16 + z * 2 + y

    def plane_copy(k, flip, d, slot):
        at = gathered.at[k, pl.ds(slot, 1)]
        return remote(
            at, at, plane_send.at[k, flip, d], plane_recv.at[k, flip, d], plane_peer(flip, d)
        )

    def x_copy(k, d, dx, x):
        at = gathered.at[k, pair_at(x, lax.rem(gz - d + 8, 8))]
        return remote(at, at, x_send.at[k, d, dx], x_recv.at[k, d, dx], x_peer(dx))

    def col_copy(k, d):
        return remote(
            parts.at[k],
            others.at[k, d],
            col_send.at[k, d],
            col_recv.at[k, d],
            (i, lax.rem(j + d, 4)),
        )

    def row_copy(k, way, d):
        col = lax.rem(j + d, 4)
        return remote(
            parts.at[k, col],
            near.at[k, way, d],
            row_send.at[k, way, d],
            row_recv.at[k, way, d],
            (lax.rem(i + (1, 63)[way], 64), col),
        )

    def basis_copy(e):
        return remote(
            modes_raw.at[:, pl.ds(512 + e * 128, 128)],
            basis_in.at[e],
            basis_send.at[e],
            basis_recv.at[e],
            beside[e ^ 1],
        )

    def gather_start(k, restricted):
        mine = slot_at(gy, gz)
        block = jnp.where(left, restricted[:16], restricted[16:])
        gathered[k, pl.ds(mine, 1)] = block.reshape(1, 16, 128)
        for d in (4, 3, 5, 2, 6, 1, 7, 0):
            for flip in (1, 0):
                if flip or d:
                    plane_copy(k, flip, d, mine).start()

        def drain(d, carry):
            plane_copy(k, 0, d, mine).wait_send()
            plane_copy(k, 1, d, mine).wait_send()
            return carry

        unsent.append(lambda: lax.fori_loop(1, 8, drain, 0))
        unsent.append(lambda: plane_copy(k, 1, 0, mine).wait_send())

    def gather_spread(k, work):
        plane_copy(k, 1, 0, slot_at(1 - gy, gz)).wait_recv()
        for dx in (2, 1, 3):
            x_copy(k, 0, dx, gx).start()

        def step(t, carry):
            d = jnp.where(lax.rem(t, 2) == 1, (t + 1) // 2, 8 - t // 2)
            z = lax.rem(gz - d + 8, 8)
            plane_copy(k, 0, d, slot_at(gy, z)).wait_recv()
            plane_copy(k, 1, d, slot_at(1 - gy, z)).wait_recv()
            for dx in (2, 1, 3):
                x_copy(k, d, dx, gx).start()
            work(t)
            return carry

        lax.fori_loop(1, 8, step, 0)

        def drain(d, carry):
            for dx in range(1, 4):
                x_copy(k, d, dx, gx).wait_send()
            return carry

        unsent.append(lambda: lax.fori_loop(0, 8, drain, 0))

    def coarse_group(k, x):
        for y in range(2):
            for zz in range(4):
                a = gathered[k, x * 16 + zz * 4 + y]
                b = gathered[k, x * 16 + zz * 4 + 2 + y]
                top = jnp.where(left, a, pltpu.roll(b, 64, 1))
                low = jnp.where(left, pltpu.roll(a, 64, 1), b)
                hi, lo = halves(jnp.concatenate([top, low], 0))
                at = pl.ds((y * 4 + zz) * 128, 128)
                x_hi[0:32, at] = hi
                x_hi[32:64, at] = lo
        at = pl.ds(pl.multiple_of(x * 1024, 1024), 1024)
        both = dot(x_hi[...], coarse_hi[:, at], NT)
        return both[:32] + both[32:] + dot(x_hi[0:32, :], coarse_lo[:, at], NT)

    def coarse_apply(k):
        part = coarse_group(k, gx)
        for dx in (1, 3, 2):
            x = lax.rem(gx - dx + 4, 4)

            def arrived(d, carry, dx=dx, x=x):
                x_copy(k, d, dx, x).wait_recv()
                return carry

            lax.fori_loop(0, 8, arrived, 0)
            part = part + coarse_group(k, x)
        for c in range(4):
            a = part[:16, (c // 2) * 128 : (c // 2) * 128 + 128]
            b = part[16:, (c // 2) * 128 : (c // 2) * 128 + 128]
            if c % 2 == 0:
                packed = jnp.where(left, a, pltpu.roll(b, 64, 1))
            else:
                packed = jnp.where(left, pltpu.roll(a, 64, 1), b)
            parts[k, c] = packed
        for d in range(4):
            for way in range(2):
                row_copy(k, way, d).start()
                unsent.append(lambda way=way, d=d: row_copy(k, way, d).wait_send())
        for d in (2, 1, 3):
            col_copy(k, d).start()
            unsent.append(lambda d=d: col_copy(k, d).wait_send())

    def coarse_finish(k):
        for d in (1, 3, 2):
            col_copy(k, d).wait_recv()
        for d in range(4):
            for way in range(2):
                row_copy(k, way, d).wait_recv()

        def in_row(col):
            return parts[k, col] + others[k, 1, col] + others[k, 2, col] + others[k, 3, col]

        def in_near(way):
            return near[k, way, 0] + near[k, way, 1] + near[k, way, 2] + near[k, way, 3]

        sums = [
            in_row(j),
            jnp.where(has[1], in_near(1), 0.0),
            jnp.where(has[0], in_near(0), 0.0),
            jnp.where(has[3], in_row(lax.rem(j + 1, 4)), 0.0),
            jnp.where(has[2], in_row(lax.rem(j + 3, 4)), 0.0),
        ]
        zero = jnp.zeros((16, 128), F32)
        rows = [
            jnp.concatenate([jnp.where(left, t, zero), jnp.where(left, zero, t)], 0) for t in sums
        ]
        return jnp.concatenate(rows, 1)

    def restrict(own, cols):
        return dot_thrice(own, modes_hi[:, cols], modes_lo[:, cols], NT)

    own_cols = slice(0, 512)
    rim_cols = slice(512, 1024)

    def pick(field):
        return dot_twice(field, pick_mat[...], NN)

    def scatter(bands):
        return dot_twice(bands, pick_t[...], NN)

    def stiff_prepare():
        loads[4].wait()
        loads[5].wait()

        def turn(t, carry):
            at = pl.ds(pl.multiple_of(t * 128, 128), 128)
            idx = jnp.concatenate([index_raw[:, at], jnp.zeros((48, 128), jnp.int32)], 0).T
            val = jnp.concatenate([coef_raw[:, at], jnp.zeros((48, 128), F32)], 0).T
            low_t[at, :] = (idx & 127).astype(F32)
            high_t[at, :] = (idx >> 7).astype(F32)
            hi = val.astype(BF).astype(F32)
            coef_hi[at, :] = hi
            coef_lo[at, :] = val - hi
            return carry

        lax.fori_loop(0, 8, turn, 0)

    def stiff_build(begin, end):
        lanes = lax.broadcasted_iota(jnp.int32, (128, 128), 0).astype(F32).astype(BF)
        blocks = lax.broadcasted_iota(jnp.int32, (8, 128), 0).astype(F32)
        one = jnp.ones((128, 128), BF)
        none = jnp.zeros((128, 128), BF)
        blank = jnp.zeros((16, 128), BF)

        def some(g, carry):
            for q in range(UNROLL // 4):
                hot = []
                val = []
                s = g * UNROLL + q * 4
                for r in range(4):
                    at = pl.ds(s + r, 1)
                    low = jnp.broadcast_to(low_t[at, :], (128, 128)).astype(BF)
                    hot.append(jnp.where(low == lanes, one, none))
                    hit = jnp.broadcast_to(high_t[at, :], (8, 128)) == blocks
                    pair = [jnp.where(hit, coef_hi[at, :], 0.0), jnp.where(hit, coef_lo[at, :], 0.0)]
                    val.append(jnp.concatenate(pair, 0).astype(BF))
                right = jnp.concatenate(
                    [jnp.concatenate(hot[:2], 1), jnp.concatenate(hot[2:], 1)], 0
                )
                rows = [
                    jnp.concatenate([val[r], blank] if r % 2 == 0 else [blank, val[r]], 1)
                    for r in range(4)
                ]
                out = dot(jnp.concatenate(rows, 0), right, NT)
                for r in range(4):
                    cut = out[16 * r : 16 * r + 16, (r // 2) * 128 : (r // 2) * 128 + 128]
                    tiles[pl.ds(pl.multiple_of((s + r) * 8, 8), 8), :] = cut[:8] + cut[8:]
            return carry

        if begin is end:
            some(begin, 0)
        else:
            lax.fori_loop(begin, end, some, 0)

    def stiff_finish():
        for r in range(4):
            for c in range(8):
                hi, lo = halves(tiles[pl.ds(c + r * 2048, 256, stride=8), :])
                stiff_hi[r * 256 : r * 256 + 256, c * 128 : c * 128 + 128] = hi
                stiff_lo[r * 256 : r * 256 + 256, c * 128 : c * 128 + 128] = lo

    def local_solve(resid, rim):
        local_buf[...] = dot_thrice(jnp.concatenate([resid, rim], 1), inv_hi[...], inv_lo[...], NT)

    def fold_basis():
        folded_hi[0:128, :] = modes_hi[:, own_cols]
        folded_lo[0:128, :] = modes_lo[:, own_cols]
        for e in range(4):
            basis_copy(e).wait_recv()
            field = dot_twice(basis_in[e], pick_t[e * 128 : (e + 1) * 128, :], NN)
            hi, lo = halves(field)
            at = slice(128 + e * 128, 256 + e * 128)
            folded_hi[at, :] = jnp.concatenate([hi, hi], 0)
            folded_lo[at, :] = jnp.concatenate([lo, lo], 0)
        lent_hi[...] = dot(folded_hi[...], pick_mat[...], NN).astype(BF)
        lent_lo[...] = dot(folded_lo[...], pick_mat[...], NN).astype(BF)

    def local_start(fold_k, resid, rim):
        local_solve(resid, rim)
        halo_start(fold_k, local_buf[:, rim_cols], 1)

    def local_finish(fold_k):
        own_buf[...] = local_buf[:, own_cols] + scatter(halo_wait(fold_k, 1))

    def nothing(*unused):
        return None

    loads[1].wait()
    rhs = rhs_ref[...]
    halo_stage(0, pick(rhs))
    stiff_prepare()
    stiff_build(0, 4)
    pl.semaphore_wait(barrier, len(greet))
    halo_send_all(0, 0)
    loads[2].wait()
    for e in range(4):
        basis_copy(e).start()
        unsent.append(lambda e=e: basis_copy(e).wait_send())

    m_hi, m_lo = halves(modes_raw[...])
    modes_hi[...] = jnp.concatenate([m_hi, m_hi], 0)
    modes_lo[...] = jnp.concatenate([m_lo, m_lo], 0)
    pick_t[...] = pick_mat[...].astype(F32).T.astype(BF)
    gram[...] = dot(pick_t[...], pick_mat[...], NN).astype(BF)
    stiff_build(4, 9)
    restricted = restrict(rhs, own_cols)
    rim = halo_wait(0, 0)
    def stiff_step(t):
        @pl.when(t < 4)
        def _():
            at = 8 + t
            stiff_build(at, at)

    gather_start(0, restricted + restrict(rim, rim_cols))
    loads[6].wait()
    split_into(inv_raw, inv_hi, inv_lo, 1024, 128)
    local_start(1, rhs, rim)
    gather_spread(0, stiff_step)
    loads[7].wait()
    split_into(coarse_raw, coarse_hi, coarse_lo, 256, 32)
    fold_basis()
    coarse_apply(0)
    local_finish(1)
    lent_buf[...] = pick(own_buf[...])
    stiff_build(12, 16)
    stiff_finish()
    spread = coarse_finish(0)
    halo_start(2, lent_buf[...] + dot_thrice(spread, lent_hi[...], lent_lo[...], NN), 0)
    first = own_buf[...] + dot_thrice(spread, folded_hi[...], folded_lo[...], NN)
    first_buf[...] = first

    part = dot_thrice(first, stiff_hi[:, own_cols], stiff_lo[:, own_cols], NT)
    loads[3].wait()
    diag = diag_ref[...]
    rim = halo_wait(2, 0)
    bands = part[:, rim_cols] + diag[:, rim_cols] * rim + dot_thrice(
        rim, stiff_hi[rim_cols, rim_cols], stiff_lo[rim_cols, rim_cols], NT
    )
    halo_start(3, bands, 1)
    own = part[:, own_cols] + diag[:, own_cols] * first + dot_thrice(
        rim, stiff_hi[own_cols, rim_cols], stiff_lo[own_cols, rim_cols], NT
    )
    own = rhs - own
    picked = pick(own)
    back = halo_wait(3, 1)
    halo_start(4, picked - dot_twice(back, gram[...], NN), 0)
    residual = own - scatter(back)
    res_buf[...] = residual
    res_copy = pltpu.make_async_copy(res_buf, res_hbm, load_sem.at[8])
    res_copy.start()
    unsent.append(res_copy.wait)

    restricted = restrict(residual, own_cols)
    rim = halo_wait(4, 0)
    gather_start(1, restricted + restrict(rim, rim_cols))
    local_start(5, residual, rim)
    gather_spread(1, nothing)
    coarse_apply(1)
    local_finish(5)
    base = first_buf[...] + own_buf[...]
    spread = coarse_finish(1)
    first_buf[...] = base + dot_thrice(spread, folded_hi[...], folded_lo[...], NN)
    sol_copy = pltpu.make_async_copy(first_buf, sol_hbm, load_sem.at[9])
    sol_copy.start()
    for finish in unsent:
        finish()
    sol_copy.wait()


def hand_on(sol_in, res_in, sol_out, res_out, sems):
    copies = [
        pltpu.make_async_copy(sol_in, sol_out, sems.at[0]),
        pltpu.make_async_copy(res_in, res_out, sems.at[1]),
    ]
    for copy in copies:
        copy.start()
    for copy in copies:
        copy.wait()


def body(
    right_side, local_inverse, modes, coarse_inverse, stiff_diag, nbr_index, nbr_coef, send_rows
):
    hbm = pl.BlockSpec(memory_space=pltpu.HBM)
    field = jax.ShapeDtypeStruct((32, 512), F32)
    dma = pltpu.SemaphoreType.DMA
    scratch = [
        pltpu.VMEM((32, 512), F32),
        pltpu.VMEM((1, 1024), F32),
        pltpu.VMEM((4, 128), jnp.int32),
        pltpu.VMEM((1024, 1024), F32),
        pltpu.VMEM((256, 4096), F32),
        pltpu.VMEM((64, 1024), F32),
        pltpu.VMEM((80, 1024), jnp.int32),
        pltpu.VMEM((80, 1024), F32),
        pltpu.VMEM((1024, 1024), BF),
        pltpu.VMEM((1024, 1024), BF),
        pltpu.VMEM((256, 4096), BF),
        pltpu.VMEM((256, 4096), BF),
        pltpu.VMEM((128, 1024), BF),
        pltpu.VMEM((128, 1024), BF),
        pltpu.VMEM((512, 512), BF),
        pltpu.VMEM((512, 512), BF),
        pltpu.VMEM((512, 512), BF),
        pltpu.VMEM((32, 512), F32),
        pltpu.VMEM((1024, 128), F32),
        pltpu.VMEM((1024, 128), F32),
        pltpu.VMEM((1024, 128), F32),
        pltpu.VMEM((1024, 128), F32),
        pltpu.VMEM((8192, 128), F32),
        pltpu.VMEM((1024, 1024), BF),
        pltpu.VMEM((1024, 1024), BF),
        pltpu.VMEM((64, 1024), BF),
        pltpu.VMEM((32, 512), F32),
        pltpu.VMEM((32, 512), F32),
        pltpu.VMEM((640, 512), BF),
        pltpu.VMEM((640, 512), BF),
        pltpu.VMEM((640, 512), BF),
        pltpu.VMEM((640, 512), BF),
        pltpu.VMEM((4, 64, 128), F32),
        pltpu.VMEM((2, 2, 4, 16, 128), F32),
        pltpu.VMEM((6, 4, 32, 128), F32),
        pltpu.VMEM((6, 4, 32, 128), F32),
        pltpu.VMEM((2, 64, 16, 128), F32),
        pltpu.VMEM((2, 4, 16, 128), F32),
        pltpu.VMEM((2, 4, 4, 16, 128), F32),
        pltpu.VMEM((32, 1024), F32),
        pltpu.VMEM((32, 512), F32),
        dma((10,)),
        dma((6, 4)),
        dma((6, 4)),
        dma((2, 2, 8)),
        dma((2, 2, 8)),
        dma((2, 8, 4)),
        dma((2, 8, 4)),
        dma((2, 4)),
        dma((2, 4)),
        dma((2, 2, 4)),
        dma((2, 2, 4)),
        dma((4,)),
        dma((4,)),
    ]
    results = tuple(
        pl.pallas_call(
            kernel,
            out_shape=(field, field),
            in_specs=[hbm] * 8,
            out_specs=(hbm, hbm),
            scratch_shapes=scratch,
            compiler_params=pltpu.CompilerParams(
                collective_id=0, has_side_effects=True, vmem_limit_bytes=60 * 2**20
            ),
            name="schwarz",
        )(
            right_side,
            local_inverse[0, 0],
            modes[0, 0],
            coarse_inverse,
            stiff_diag[0],
            nbr_index[0, 0],
            nbr_coef[0, 0],
            send_rows[0, 0],
        )
    )
    return tuple(
        pl.pallas_call(
            hand_on,
            out_shape=(field, field),
            in_specs=[hbm] * 2,
            out_specs=(hbm, hbm),
            scratch_shapes=[dma((2,))],
            name="results",
        )(*results)
    )


def solution(mesh):
    in_specs = (
        P(None, ("rows", "cols")),
        P("rows", "cols", None, None),
        P("rows", "cols", None, None),
        P("rows", "cols"),
        P("rows", "cols", None),
        P("rows", "cols", None, None),
        P("rows", "cols", None, None),
        P("rows", "cols", None, None),
    )
    out_specs = (P(None, ("rows", "cols")), P(None, ("rows", "cols")))
    return jax.shard_map(body, mesh=mesh, in_specs=in_specs, out_specs=out_specs, check_vma=False)
```

```python
import jax
import jax.numpy as jnp
from jax import lax
from jax.experimental import pallas as pl
from jax.experimental.pallas import tpu as pltpu
from jax.sharding import PartitionSpec as P

BF = jnp.bfloat16
F32 = jnp.float32
NT = (((1,), (1,)), ((), ()))
NN = (((1,), (0,)), ((), ()))
UNROLL = 32


def dot(a, b, dims):
    return lax.dot_general(a, b, dims, preferred_element_type=F32)


def halves(x):
    hi = x.astype(BF)
    return hi, (x - hi.astype(F32)).astype(BF)


def split_into(src, high, low, rows, step):
    def part(t, carry):
        at = pl.ds(pl.multiple_of(t * step, step), step)
        hi, lo = halves(src[at, :])
        high[at, :] = hi
        low[at, :] = lo
        return carry

    lax.fori_loop(0, rows // step, part, 0)


def dot_twice(x, w, dims):
    n = x.shape[0]
    hi, lo = halves(x)
    both = dot(jnp.concatenate([hi, lo], 0), w, dims)
    return both[:n] + both[n:]


def dot_thrice(x, high, low, dims):
    n = x.shape[0]
    hi, lo = halves(x)
    both = dot(jnp.concatenate([hi, lo], 0), high, dims)
    return both[:n] + both[n:] + dot(hi, low, dims)


def kernel(
    rhs_hbm, inv_hbm, modes_hbm, coarse_hbm, diag_hbm, index_hbm, coef_hbm, sends_hbm,
    sol_ref, res_ref,
    rhs_ref, diag_ref, sends_ref, inv_raw, coarse_raw, modes_raw, index_raw, coef_raw,
    inv_hi, inv_lo, coarse_hi, coarse_lo, modes_hi, modes_lo,
    pick_mat, pick_t, gram, low_t, high_t, coef_hi, coef_lo, tiles, stiff_hi, stiff_lo,
    x_hi, own_buf, lent_buf, folded_hi, folded_lo, lent_hi, lent_lo, basis_in, near, halo_out, halo_in, gathered, parts, others, local_buf, first_buf,
    load_sem, halo_send, halo_recv, plane_send, plane_recv, x_send, x_recv,
    col_send, col_recv, row_send, row_recv, basis_send, basis_recv,
):
    i = lax.axis_index("rows")
    j = lax.axis_index("cols")
    gx = i // 16
    gy = lax.rem(i // 8, 2)
    gz = lax.rem(i, 8)

    def row_of(x, y, z):
        return x * 16 + y * 8 + z

    loads = [
        pltpu.make_async_copy(s, d, load_sem.at[n])
        for n, (s, d) in enumerate(
            [
                (sends_hbm, sends_ref),
                (rhs_hbm, rhs_ref),
                (modes_hbm, modes_raw),
                (diag_hbm, diag_ref),
                (index_hbm, index_raw),
                (coef_hbm, coef_raw),
                (inv_hbm, inv_raw),
                (coarse_hbm, coarse_raw),
            ]
        )
    ]
    for load in loads:
        load.start()

    beside = [
        (lax.rem(i + 1, 64), j),
        (lax.rem(i + 63, 64), j),
        (i, lax.rem(j + 1, 4)),
        (i, lax.rem(j + 3, 4)),
    ]

    def plane_peer(flip, d):
        return (row_of(gx, 1 - gy if flip else gy, lax.rem(gz + d, 8)), j)

    def x_peer(d):
        return (row_of(lax.rem(gx + d, 4), gy, gz), j)

    unsent = []
    barrier = pltpu.get_barrier_semaphore()
    greet = [plane_peer(flip, d) for d in (4, 3, 5, 2, 6, 1, 7, 0) for flip in (1, 0) if flip or d]
    greet = greet + [x_peer(d) for d in (2, 1, 3)] + [(i, lax.rem(j + d, 4)) for d in (2, 1, 3)]
    greet = greet + [(lax.rem(i + way, 64), lax.rem(j + d, 4)) for way in (1, 63) for d in range(4)]
    for peer in greet:
        pl.semaphore_signal(barrier, inc=1, device_id=peer, device_id_type=pl.DeviceIdType.MESH)

    loads[0].wait()
    row_ids = lax.broadcasted_iota(jnp.int32, (512, 128), 0)
    for e in range(4):
        hit = row_ids == jnp.broadcast_to(sends_ref[e : e + 1, :], (512, 128))
        pick_mat[:, e * 128 : (e + 1) * 128] = jnp.where(hit, 1.0, 0.0).astype(BF)

    has = [i > 0, i < 63, j > 0, j < 3]

    def halo_copy(k, e, way):
        return pltpu.make_async_remote_copy(
            src_ref=halo_out.at[k, e],
            dst_ref=halo_in.at[k, e],
            send_sem=halo_send.at[k, e],
            recv_sem=halo_recv.at[k, e],
            device_id=beside[way],
            device_id_type=pl.DeviceIdType.MESH,
        )

    def halo_stage(k, values):
        for e in range(4):
            halo_out[k, e] = values[:, e * 128 : (e + 1) * 128]

    def halo_send_all(k, back):
        for e in range(4):
            halo_copy(k, e, e ^ back).start()
            unsent.append(lambda e=e: halo_copy(k, e, e ^ back).wait_send())

    def halo_start(k, values, back):
        halo_stage(k, values)
        halo_send_all(k, back)

    def halo_wait(k, back):
        got = []
        for e in range(4):
            halo_copy(k, e, e ^ back).wait_recv()
            got.append(jnp.where(has[e ^ back], halo_in[k, e], 0.0))
        return jnp.concatenate(got, 1)

    lane = lax.broadcasted_iota(jnp.int32, (16, 128), 1)
    left = lane < 64

    def pair_at(x, z):
        return pl.ds(x * 16 + z * 2, 2)

    def remote(src, dst, send, recv, peer):
        return pltpu.make_async_remote_copy(
            src_ref=src,
            dst_ref=dst,
            send_sem=send,
            recv_sem=recv,
            device_id=peer,
            device_id_type=pl.DeviceIdType.MESH,
        )

    def slot_at(y, z):
        return gx * 16 + z * 2 + y

    def plane_copy(k, flip, d, slot):
        at = gathered.at[k, pl.ds(slot, 1)]
        return remote(
            at, at, plane_send.at[k, flip, d], plane_recv.at[k, flip, d], plane_peer(flip, d)
        )

    def x_copy(k, d, dx, x):
        at = gathered.at[k, pair_at(x, lax.rem(gz - d + 8, 8))]
        return remote(at, at, x_send.at[k, d, dx], x_recv.at[k, d, dx], x_peer(dx))

    def col_copy(k, d):
        return remote(
            parts.at[k],
            others.at[k, d],
            col_send.at[k, d],
            col_recv.at[k, d],
            (i, lax.rem(j + d, 4)),
        )

    def row_copy(k, way, d):
        col = lax.rem(j + d, 4)
        return remote(
            parts.at[k, col],
            near.at[k, way, d],
            row_send.at[k, way, d],
            row_recv.at[k, way, d],
            (lax.rem(i + (1, 63)[way], 64), col),
        )

    def basis_copy(e):
        return remote(
            modes_raw.at[:, pl.ds(512 + e * 128, 128)],
            basis_in.at[e],
            basis_send.at[e],
            basis_recv.at[e],
            beside[e ^ 1],
        )

    def gather_start(k, restricted):
        mine = slot_at(gy, gz)
        block = jnp.where(left, restricted[:16], restricted[16:])
        gathered[k, pl.ds(mine, 1)] = block.reshape(1, 16, 128)
        for d in (4, 3, 5, 2, 6, 1, 7, 0):
            for flip in (1, 0):
                if flip or d:
                    plane_copy(k, flip, d, mine).start()

        def drain(d, carry):
            plane_copy(k, 0, d, mine).wait_send()
            plane_copy(k, 1, d, mine).wait_send()
            return carry

        unsent.append(lambda: lax.fori_loop(1, 8, drain, 0))
        unsent.append(lambda: plane_copy(k, 1, 0, mine).wait_send())

    def gather_spread(k, work):
        plane_copy(k, 1, 0, slot_at(1 - gy, gz)).wait_recv()
        for dx in (2, 1, 3):
            x_copy(k, 0, dx, gx).start()

        def step(t, carry):
            d = jnp.where(lax.rem(t, 2) == 1, (t + 1) // 2, 8 - t // 2)
            z = lax.rem(gz - d + 8, 8)
            plane_copy(k, 0, d, slot_at(gy, z)).wait_recv()
            plane_copy(k, 1, d, slot_at(1 - gy, z)).wait_recv()
            for dx in (2, 1, 3):
                x_copy(k, d, dx, gx).start()
            work(t)
            return carry

        lax.fori_loop(1, 8, step, 0)

        def drain(d, carry):
            for dx in range(1, 4):
                x_copy(k, d, dx, gx).wait_send()
            return carry

        unsent.append(lambda: lax.fori_loop(0, 8, drain, 0))

    def coarse_group(k, x):
        for y in range(2):
            for zz in range(4):
                a = gathered[k, x * 16 + zz * 4 + y]
                b = gathered[k, x * 16 + zz * 4 + 2 + y]
                top = jnp.where(left, a, pltpu.roll(b, 64, 1))
                low = jnp.where(left, pltpu.roll(a, 64, 1), b)
                hi, lo = halves(jnp.concatenate([top, low], 0))
                at = pl.ds((y * 4 + zz) * 128, 128)
                x_hi[0:32, at] = hi
                x_hi[32:64, at] = lo
        at = pl.ds(pl.multiple_of(x * 1024, 1024), 1024)
        both = dot(x_hi[...], coarse_hi[:, at], NT)
        return both[:32] + both[32:] + dot(x_hi[0:32, :], coarse_lo[:, at], NT)

    def coarse_apply(k):
        part = coarse_group(k, gx)
        for dx in (1, 3, 2):
            x = lax.rem(gx - dx + 4, 4)

            def arrived(d, carry, dx=dx, x=x):
                x_copy(k, d, dx, x).wait_recv()
                return carry

            lax.fori_loop(0, 8, arrived, 0)
            part = part + coarse_group(k, x)
        for c in range(4):
            a = part[:16, (c // 2) * 128 : (c // 2) * 128 + 128]
            b = part[16:, (c // 2) * 128 : (c // 2) * 128 + 128]
            if c % 2 == 0:
                packed = jnp.where(left, a, pltpu.roll(b, 64, 1))
            else:
                packed = jnp.where(left, pltpu.roll(a, 64, 1), b)
            parts[k, c] = packed
        for d in range(4):
            for way in range(2):
                row_copy(k, way, d).start()
                unsent.append(lambda way=way, d=d: row_copy(k, way, d).wait_send())
        for d in (2, 1, 3):
            col_copy(k, d).start()
            unsent.append(lambda d=d: col_copy(k, d).wait_send())

    def coarse_finish(k):
        for d in (1, 3, 2):
            col_copy(k, d).wait_recv()
        for d in range(4):
            for way in range(2):
                row_copy(k, way, d).wait_recv()

        def in_row(col):
            return parts[k, col] + others[k, 1, col] + others[k, 2, col] + others[k, 3, col]

        def in_near(way):
            return near[k, way, 0] + near[k, way, 1] + near[k, way, 2] + near[k, way, 3]

        sums = [
            in_row(j),
            jnp.where(has[1], in_near(1), 0.0),
            jnp.where(has[0], in_near(0), 0.0),
            jnp.where(has[3], in_row(lax.rem(j + 1, 4)), 0.0),
            jnp.where(has[2], in_row(lax.rem(j + 3, 4)), 0.0),
        ]
        zero = jnp.zeros((16, 128), F32)
        rows = [
            jnp.concatenate([jnp.where(left, t, zero), jnp.where(left, zero, t)], 0) for t in sums
        ]
        return jnp.concatenate(rows, 1)

    def restrict(own, cols):
        return dot_thrice(own, modes_hi[:, cols], modes_lo[:, cols], NT)

    own_cols = slice(0, 512)
    rim_cols = slice(512, 1024)

    def pick(field):
        return dot_twice(field, pick_mat[...], NN)

    def scatter(bands):
        return dot_twice(bands, pick_t[...], NN)

    def stiff_prepare():
        loads[4].wait()
        loads[5].wait()

        for t in range(3):
            def stack(raw, dtype):
                rows = [
                    raw[:, p * 384 + t * 128 : p * 384 + t * 128 + 128]
                    if p * 384 + t * 128 < 1024
                    else jnp.zeros((80, 128), dtype)
                    for p in range(3)
                ]
                rows.append(jnp.zeros((16, 128), dtype))
                return jnp.concatenate(rows, 0).T

            at = slice(t * 128, t * 128 + 128)
            idx = stack(index_raw, jnp.int32)
            val = stack(coef_raw, F32)
            low_t[at, :] = (idx & 127).astype(F32)
            high_t[at, :] = (idx >> 7).astype(F32)
            hi = val.astype(BF).astype(F32)
            coef_hi[at, :] = hi
            coef_lo[at, :] = val - hi

    def stiff_build(begin, end):
        lanes = lax.broadcasted_iota(jnp.int32, (128, 256), 0).astype(F32).astype(BF)
        blocks = lax.broadcasted_iota(jnp.int32, (8, 256), 0).astype(F32)
        one = jnp.ones((128, 256), BF)
        none = jnp.zeros((128, 256), BF)
        third = lax.broadcasted_iota(jnp.int32, (8, 256), 1) // 80

        def some(g, carry):
            for q in range(UNROLL // 2):
                hot = []
                val = []
                s = g * UNROLL + q * 2
                for r in range(2):
                    at = pl.ds(s + r, 1)
                    low = jnp.broadcast_to(low_t[at, :], (128, 256)).astype(BF)
                    hot.append(jnp.where(low == lanes, one, none))
                    hit = jnp.broadcast_to(high_t[at, :], (8, 256)) == blocks
                    high = jnp.where(hit, coef_hi[at, :], 0.0)
                    rest = jnp.where(hit, coef_lo[at, :], 0.0)
                    for p in range(3):
                        pair = [jnp.where(third == p, high, 0.0), jnp.where(third == p, rest, 0.0)]
                        val.append(jnp.concatenate(pair, 0).astype(BF))
                out = dot(jnp.concatenate(val, 0), jnp.concatenate(hot, 0), NT)
                for r in range(2):
                    for p in range(3):
                        cut = out[(r * 3 + p) * 16 : (r * 3 + p) * 16 + 16, r * 128 : r * 128 + 128]
                        row = (p * 384 + s + r) * 8
                        tiles[pl.ds(pl.multiple_of(row, 8), 8), :] = cut[:8] + cut[8:]
            return carry

        if begin is end:
            some(begin, 0)
        else:
            lax.fori_loop(begin, end, some, 0)

    def stiff_finish():
        for r in range(4):
            for c in range(8):
                hi, lo = halves(tiles[pl.ds(c + r * 2048, 256, stride=8), :])
                stiff_hi[r * 256 : r * 256 + 256, c * 128 : c * 128 + 128] = hi
                stiff_lo[r * 256 : r * 256 + 256, c * 128 : c * 128 + 128] = lo

    def local_solve(resid, rim):
        local_buf[...] = dot_thrice(jnp.concatenate([resid, rim], 1), inv_hi[...], inv_lo[...], NT)

    def fold_basis():
        folded_hi[0:128, :] = modes_hi[:, own_cols]
        folded_lo[0:128, :] = modes_lo[:, own_cols]
        for e in range(4):
            basis_copy(e).wait_recv()
            field = dot_twice(basis_in[e], pick_t[e * 128 : (e + 1) * 128, :], NN)
            hi, lo = halves(field)
            at = slice(128 + e * 128, 256 + e * 128)
            folded_hi[at, :] = jnp.concatenate([hi, hi], 0)
            folded_lo[at, :] = jnp.concatenate([lo, lo], 0)
        lent_hi[...] = dot(folded_hi[...], pick_mat[...], NN).astype(BF)
        lent_lo[...] = dot(folded_lo[...], pick_mat[...], NN).astype(BF)

    def local_start(fold_k, resid, rim):
        local_solve(resid, rim)
        halo_start(fold_k, local_buf[:, rim_cols], 1)

    def local_finish(fold_k):
        own_buf[...] = local_buf[:, own_cols] + scatter(halo_wait(fold_k, 1))

    def nothing(*unused):
        return None

    loads[1].wait()
    rhs = rhs_ref[...]
    halo_stage(0, pick(rhs))
    stiff_prepare()
    stiff_build(0, 4)
    pl.semaphore_wait(barrier, len(greet))
    halo_send_all(0, 0)
    loads[2].wait()
    for e in range(4):
        basis_copy(e).start()
        unsent.append(lambda e=e: basis_copy(e).wait_send())

    m_hi, m_lo = halves(modes_raw[...])
    modes_hi[...] = jnp.concatenate([m_hi, m_hi], 0)
    modes_lo[...] = jnp.concatenate([m_lo, m_lo], 0)
    columns = jnp.concatenate([sends_ref[...], sends_ref[...]], 0).T
    lane_ids = lax.broadcasted_iota(jnp.int32, (128, 512), 1)
    for e in range(4):
        column = columns[:, e : e + 1]
        at = slice(e * 128, e * 128 + 128)
        hit = jnp.broadcast_to(column, (128, 512)) == lane_ids
        pick_t[at, :] = jnp.where(hit, 1.0, 0.0).astype(BF)
        for f in range(4):
            row = jnp.broadcast_to(sends_ref[f : f + 1, :], (128, 128))
            hit = jnp.broadcast_to(column, (128, 128)) == row
            gram[at, f * 128 : f * 128 + 128] = jnp.where(hit, 1.0, 0.0).astype(BF)
    stiff_build(4, 8)
    restricted = restrict(rhs, own_cols)
    rim = halo_wait(0, 0)
    def stiff_step(t):
        @pl.when(t == 1)
        def _():
            at = 7 + t
            stiff_build(at, at)

    gather_start(0, restricted + restrict(rim, rim_cols))
    loads[6].wait()
    split_into(inv_raw, inv_hi, inv_lo, 1024, 128)
    local_start(1, rhs, rim)
    gather_spread(0, stiff_step)
    loads[7].wait()
    split_into(coarse_raw, coarse_hi, coarse_lo, 256, 32)
    fold_basis()
    coarse_apply(0)
    local_finish(1)
    lent_buf[...] = pick(own_buf[...])
    stiff_build(9, 12)
    stiff_finish()
    spread = coarse_finish(0)
    halo_start(2, lent_buf[...] + dot_thrice(spread, lent_hi[...], lent_lo[...], NN), 0)
    first = own_buf[...] + dot_thrice(spread, folded_hi[...], folded_lo[...], NN)
    first_buf[...] = first

    part = dot_thrice(first, stiff_hi[:, own_cols], stiff_lo[:, own_cols], NT)
    loads[3].wait()
    diag = diag_ref[...]
    rim = halo_wait(2, 0)
    bands = part[:, rim_cols] + diag[:, rim_cols] * rim + dot_thrice(
        rim, stiff_hi[rim_cols, rim_cols], stiff_lo[rim_cols, rim_cols], NT
    )
    halo_start(3, bands, 1)
    own = part[:, own_cols] + diag[:, own_cols] * first + dot_thrice(
        rim, stiff_hi[own_cols, rim_cols], stiff_lo[own_cols, rim_cols], NT
    )
    own = rhs - own
    picked = pick(own)
    back = halo_wait(3, 1)
    halo_start(4, picked - dot_twice(back, gram[...], NN), 0)
    residual = own - scatter(back)
    res_ref[...] = residual

    restricted = restrict(residual, own_cols)
    rim = halo_wait(4, 0)
    gather_start(1, restricted + restrict(rim, rim_cols))
    local_start(5, residual, rim)
    gather_spread(1, nothing)
    coarse_apply(1)
    local_finish(5)
    base = first_buf[...] + own_buf[...]
    spread = coarse_finish(1)
    sol_ref[...] = base + dot_thrice(spread, folded_hi[...], folded_lo[...], NN)
    for finish in unsent:
        finish()


def body(
    right_side, local_inverse, modes, coarse_inverse, stiff_diag, nbr_index, nbr_coef, send_rows
):
    hbm = pl.BlockSpec(memory_space=pltpu.HBM)
    field = pltpu.VMEM((32, 512), F32)
    vmem = pl.BlockSpec(memory_space=pltpu.VMEM)
    dma = pltpu.SemaphoreType.DMA
    scratch = [
        pltpu.VMEM((32, 512), F32),
        pltpu.VMEM((1, 1024), F32),
        pltpu.VMEM((4, 128), jnp.int32),
        pltpu.VMEM((1024, 1024), F32),
        pltpu.VMEM((256, 4096), F32),
        pltpu.VMEM((64, 1024), F32),
        pltpu.VMEM((80, 1024), jnp.int32),
        pltpu.VMEM((80, 1024), F32),
        pltpu.VMEM((1024, 1024), BF),
        pltpu.VMEM((1024, 1024), BF),
        pltpu.VMEM((256, 4096), BF),
        pltpu.VMEM((256, 4096), BF),
        pltpu.VMEM((128, 1024), BF),
        pltpu.VMEM((128, 1024), BF),
        pltpu.VMEM((512, 512), BF),
        pltpu.VMEM((512, 512), BF),
        pltpu.VMEM((512, 512), BF),
        pltpu.VMEM((384, 256), F32),
        pltpu.VMEM((384, 256), F32),
        pltpu.VMEM((384, 256), F32),
        pltpu.VMEM((384, 256), F32),
        pltpu.VMEM((9216, 128), F32),
        pltpu.VMEM((1024, 1024), BF),
        pltpu.VMEM((1024, 1024), BF),
        pltpu.VMEM((64, 1024), BF),
        pltpu.VMEM((32, 512), F32),
        pltpu.VMEM((32, 512), F32),
        pltpu.VMEM((640, 512), BF),
        pltpu.VMEM((640, 512), BF),
        pltpu.VMEM((640, 512), BF),
        pltpu.VMEM((640, 512), BF),
        pltpu.VMEM((4, 64, 128), F32),
        pltpu.VMEM((2, 2, 4, 16, 128), F32),
        pltpu.VMEM((6, 4, 32, 128), F32),
        pltpu.VMEM((6, 4, 32, 128), F32),
        pltpu.VMEM((2, 64, 16, 128), F32),
        pltpu.VMEM((2, 4, 16, 128), F32),
        pltpu.VMEM((2, 4, 4, 16, 128), F32),
        pltpu.VMEM((32, 1024), F32),
        pltpu.VMEM((32, 512), F32),
        dma((8,)),
        dma((6, 4)),
        dma((6, 4)),
        dma((2, 2, 8)),
        dma((2, 2, 8)),
        dma((2, 8, 4)),
        dma((2, 8, 4)),
        dma((2, 4)),
        dma((2, 4)),
        dma((2, 2, 4)),
        dma((2, 2, 4)),
        dma((4,)),
        dma((4,)),
    ]
    return tuple(
        pl.pallas_call(
            kernel,
            out_shape=(field, field),
            in_specs=[hbm] * 8,
            out_specs=(vmem, vmem),
            scratch_shapes=scratch,
            compiler_params=pltpu.CompilerParams(
                collective_id=0, has_side_effects=True, vmem_limit_bytes=60 * 2**20
            ),
            name="schwarz",
        )(
            right_side,
            local_inverse[0, 0],
            modes[0, 0],
            coarse_inverse,
            stiff_diag[0],
            nbr_index[0, 0],
            nbr_coef[0, 0],
            send_rows[0, 0],
        )
    )


def solution(mesh):
    in_specs = (
        P(None, ("rows", "cols")),
        P("rows", "cols", None, None),
        P("rows", "cols", None, None),
        P("rows", "cols"),
        P("rows", "cols", None),
        P("rows", "cols", None, None),
        P("rows", "cols", None, None),
        P("rows", "cols", None, None),
    )
    out_specs = (P(None, ("rows", "cols")), P(None, ("rows", "cols")))
    return jax.shard_map(body, mesh=mesh, in_specs=in_specs, out_specs=out_specs, check_vma=False)
```

```python
import jax
import jax.numpy as jnp
from jax import lax
from jax.experimental import pallas as pl
from jax.experimental.pallas import tpu as pltpu
from jax.sharding import PartitionSpec as P

BF = jnp.bfloat16
F32 = jnp.float32
NT = (((1,), (1,)), ((), ()))
NN = (((1,), (0,)), ((), ()))
UNROLL = 32


def dot(a, b, dims):
    return lax.dot_general(a, b, dims, preferred_element_type=F32)


def halves(x):
    hi = x.astype(BF)
    return hi, (x - hi.astype(F32)).astype(BF)


def split_into(src, high, low, rows, step):
    def part(t, carry):
        at = pl.ds(pl.multiple_of(t * step, step), step)
        hi, lo = halves(src[at, :])
        high[at, :] = hi
        low[at, :] = lo
        return carry

    lax.fori_loop(0, rows // step, part, 0)


def dot_twice(x, w, dims):
    n = x.shape[0]
    hi, lo = halves(x)
    both = dot(jnp.concatenate([hi, lo], 0), w, dims)
    return both[:n] + both[n:]


def dot_thrice(x, high, low, dims):
    n = x.shape[0]
    hi, lo = halves(x)
    both = dot(jnp.concatenate([hi, lo], 0), high, dims)
    return both[:n] + both[n:] + dot(hi, low, dims)


def kernel(
    rhs_hbm, inv_hbm, modes_hbm, coarse_hbm, diag_hbm, index_hbm, coef_hbm, sends_hbm,
    sol_ref, res_ref,
    rhs_ref, diag_ref, sends_ref, inv_raw, coarse_raw, modes_raw, index_raw, coef_raw,
    inv_hi, inv_lo, coarse_hi, coarse_lo, modes_hi, modes_lo,
    pick_mat, pick_t, gram, low_t, high_t, coef_hi, coef_lo, tiles, stiff_hi, stiff_lo,
    x_hi, own_buf, lent_buf, folded_hi, folded_lo, lent_hi, lent_lo, basis_in, near, halo_out, halo_in, gathered, parts, others, local_buf, first_buf,
    load_sem, halo_send, halo_recv, plane_send, plane_recv, x_send, x_recv,
    col_send, col_recv, row_send, row_recv, basis_send, basis_recv,
):
    i = lax.axis_index("rows")
    j = lax.axis_index("cols")
    gx = i // 16
    gy = lax.rem(i // 8, 2)
    gz = lax.rem(i, 8)

    def row_of(x, y, z):
        return x * 16 + y * 8 + z

    loads = [
        pltpu.make_async_copy(s, d, load_sem.at[n])
        for n, (s, d) in enumerate(
            [
                (sends_hbm, sends_ref),
                (rhs_hbm, rhs_ref),
                (modes_hbm, modes_raw),
                (diag_hbm, diag_ref),
                (index_hbm, index_raw),
                (coef_hbm, coef_raw),
                (inv_hbm, inv_raw),
                (coarse_hbm, coarse_raw),
            ]
        )
    ]
    for load in loads:
        load.start()

    beside = [
        (lax.rem(i + 1, 64), j),
        (lax.rem(i + 63, 64), j),
        (i, lax.rem(j + 1, 4)),
        (i, lax.rem(j + 3, 4)),
    ]

    def plane_peer(flip, d):
        return (row_of(gx, 1 - gy if flip else gy, lax.rem(gz + d, 8)), j)

    def x_peer(d):
        return (row_of(lax.rem(gx + d, 4), gy, gz), j)

    unsent = []
    barrier = pltpu.get_barrier_semaphore()
    greet = [plane_peer(flip, d) for d in (4, 3, 5, 2, 6, 1, 7, 0) for flip in (1, 0) if flip or d]
    greet = greet + [x_peer(d) for d in (2, 1, 3)] + [(i, lax.rem(j + d, 4)) for d in (2, 1, 3)]
    greet = greet + [(lax.rem(i + way, 64), lax.rem(j + d, 4)) for way in (1, 63) for d in range(4)]
    for peer in greet:
        pl.semaphore_signal(barrier, inc=1, device_id=peer, device_id_type=pl.DeviceIdType.MESH)

    loads[0].wait()
    row_ids = lax.broadcasted_iota(jnp.int32, (512, 128), 0)
    for e in range(4):
        hit = row_ids == jnp.broadcast_to(sends_ref[e : e + 1, :], (512, 128))
        pick_mat[:, e * 128 : (e + 1) * 128] = jnp.where(hit, 1.0, 0.0).astype(BF)

    has = [i > 0, i < 63, j > 0, j < 3]

    def halo_copy(k, e, way):
        return pltpu.make_async_remote_copy(
            src_ref=halo_out.at[k, e],
            dst_ref=halo_in.at[k, e],
            send_sem=halo_send.at[k, e],
            recv_sem=halo_recv.at[k, e],
            device_id=beside[way],
            device_id_type=pl.DeviceIdType.MESH,
        )

    def halo_stage(k, values):
        for e in range(4):
            halo_out[k, e] = values[:, e * 128 : (e + 1) * 128]

    def halo_send_all(k, back):
        for e in range(4):
            halo_copy(k, e, e ^ back).start()
            unsent.append(lambda e=e: halo_copy(k, e, e ^ back).wait_send())

    def halo_start(k, values, back):
        halo_stage(k, values)
        halo_send_all(k, back)

    def halo_wait(k, back):
        got = []
        for e in range(4):
            halo_copy(k, e, e ^ back).wait_recv()
            got.append(jnp.where(has[e ^ back], halo_in[k, e], 0.0))
        return jnp.concatenate(got, 1)

    lane = lax.broadcasted_iota(jnp.int32, (16, 128), 1)
    left = lane < 64

    def pair_at(x, z):
        return pl.ds(x * 16 + z * 2, 2)

    def remote(src, dst, send, recv, peer):
        return pltpu.make_async_remote_copy(
            src_ref=src,
            dst_ref=dst,
            send_sem=send,
            recv_sem=recv,
            device_id=peer,
            device_id_type=pl.DeviceIdType.MESH,
        )

    def slot_at(y, z):
        return gx * 16 + z * 2 + y

    def plane_copy(k, flip, d, slot):
        at = gathered.at[k, pl.ds(slot, 1)]
        return remote(
            at, at, plane_send.at[k, flip, d], plane_recv.at[k, flip, d], plane_peer(flip, d)
        )

    def x_copy(k, d, dx, x):
        at = gathered.at[k, pair_at(x, lax.rem(gz - d + 8, 8))]
        return remote(at, at, x_send.at[k, d, dx], x_recv.at[k, d, dx], x_peer(dx))

    def col_copy(k, d):
        return remote(
            parts.at[k],
            others.at[k, d],
            col_send.at[k, d],
            col_recv.at[k, d],
            (i, lax.rem(j + d, 4)),
        )

    def row_copy(k, way, d):
        col = lax.rem(j + d, 4)
        return remote(
            parts.at[k, col],
            near.at[k, way, d],
            row_send.at[k, way, d],
            row_recv.at[k, way, d],
            (lax.rem(i + (1, 63)[way], 64), col),
        )

    def basis_copy(e):
        return remote(
            modes_raw.at[:, pl.ds(512 + e * 128, 128)],
            basis_in.at[e],
            basis_send.at[e],
            basis_recv.at[e],
            beside[e ^ 1],
        )

    def gather_start(k, restricted):
        mine = slot_at(gy, gz)
        block = jnp.where(left, restricted[:16], restricted[16:])
        gathered[k, pl.ds(mine, 1)] = block.reshape(1, 16, 128)
        for d in (0, 1, 7, 2, 6, 3, 5, 4):
            for flip in (1, 0):
                if flip or d:
                    plane_copy(k, flip, d, mine).start()

        def drain(d, carry):
            plane_copy(k, 0, d, mine).wait_send()
            plane_copy(k, 1, d, mine).wait_send()
            return carry

        unsent.append(lambda: lax.fori_loop(1, 8, drain, 0))
        unsent.append(lambda: plane_copy(k, 1, 0, mine).wait_send())

    def gather_spread(k, work):
        plane_copy(k, 1, 0, slot_at(1 - gy, gz)).wait_recv()
        for dx in (2, 1, 3):
            x_copy(k, 0, dx, gx).start()

        def step(t, carry):
            d = jnp.where(lax.rem(t, 2) == 1, (t + 1) // 2, 8 - t // 2)
            z = lax.rem(gz - d + 8, 8)
            plane_copy(k, 0, d, slot_at(gy, z)).wait_recv()
            plane_copy(k, 1, d, slot_at(1 - gy, z)).wait_recv()
            for dx in (2, 1, 3):
                x_copy(k, d, dx, gx).start()
            work(t)
            return carry

        lax.fori_loop(1, 8, step, 0)

        def drain(d, carry):
            for dx in range(1, 4):
                x_copy(k, d, dx, gx).wait_send()
            return carry

        unsent.append(lambda: lax.fori_loop(0, 8, drain, 0))

    def coarse_group(k, x):
        for y in range(2):
            for zz in range(4):
                a = gathered[k, x * 16 + zz * 4 + y]
                b = gathered[k, x * 16 + zz * 4 + 2 + y]
                top = jnp.where(left, a, pltpu.roll(b, 64, 1))
                low = jnp.where(left, pltpu.roll(a, 64, 1), b)
                hi, lo = halves(jnp.concatenate([top, low], 0))
                at = pl.ds((y * 4 + zz) * 128, 128)
                x_hi[0:32, at] = hi
                x_hi[32:64, at] = lo
        at = pl.ds(pl.multiple_of(x * 1024, 1024), 1024)
        both = dot(x_hi[...], coarse_hi[:, at], NT)
        return both[:32] + both[32:] + dot(x_hi[0:32, :], coarse_lo[:, at], NT)

    def coarse_apply(k):
        part = coarse_group(k, gx)
        for dx in (1, 3, 2):
            x = lax.rem(gx - dx + 4, 4)

            def arrived(d, carry, dx=dx, x=x):
                x_copy(k, d, dx, x).wait_recv()
                return carry

            lax.fori_loop(0, 8, arrived, 0)
            part = part + coarse_group(k, x)
        for c in range(4):
            a = part[:16, (c // 2) * 128 : (c // 2) * 128 + 128]
            b = part[16:, (c // 2) * 128 : (c // 2) * 128 + 128]
            if c % 2 == 0:
                packed = jnp.where(left, a, pltpu.roll(b, 64, 1))
            else:
                packed = jnp.where(left, pltpu.roll(a, 64, 1), b)
            parts[k, c] = packed
        for d in range(4):
            for way in range(2):
                row_copy(k, way, d).start()
                unsent.append(lambda way=way, d=d: row_copy(k, way, d).wait_send())
        for d in (2, 1, 3):
            col_copy(k, d).start()
            unsent.append(lambda d=d: col_copy(k, d).wait_send())

    def coarse_finish(k):
        for d in (1, 3, 2):
            col_copy(k, d).wait_recv()
        for d in range(4):
            for way in range(2):
                row_copy(k, way, d).wait_recv()

        def in_row(col):
            return parts[k, col] + others[k, 1, col] + others[k, 2, col] + others[k, 3, col]

        def in_near(way):
            return near[k, way, 0] + near[k, way, 1] + near[k, way, 2] + near[k, way, 3]

        sums = [
            in_row(j),
            jnp.where(has[1], in_near(1), 0.0),
            jnp.where(has[0], in_near(0), 0.0),
            jnp.where(has[3], in_row(lax.rem(j + 1, 4)), 0.0),
            jnp.where(has[2], in_row(lax.rem(j + 3, 4)), 0.0),
        ]
        zero = jnp.zeros((16, 128), F32)
        rows = [
            jnp.concatenate([jnp.where(left, t, zero), jnp.where(left, zero, t)], 0) for t in sums
        ]
        return jnp.concatenate(rows, 1)

    def restrict(own, cols):
        return dot_thrice(own, modes_hi[:, cols], modes_lo[:, cols], NT)

    own_cols = slice(0, 512)
    rim_cols = slice(512, 1024)

    def pick(field):
        return dot_twice(field, pick_mat[...], NN)

    def scatter(bands):
        return dot_twice(bands, pick_t[...], NN)

    def stiff_prepare():
        loads[4].wait()
        loads[5].wait()

        for t in range(3):
            def stack(raw, dtype):
                rows = [
                    raw[:, p * 384 + t * 128 : p * 384 + t * 128 + 128]
                    if p * 384 + t * 128 < 1024
                    else jnp.zeros((80, 128), dtype)
                    for p in range(3)
                ]
                rows.append(jnp.zeros((16, 128), dtype))
                return jnp.concatenate(rows, 0).T

            at = slice(t * 128, t * 128 + 128)
            idx = stack(index_raw, jnp.int32)
            val = stack(coef_raw, F32)
            low_t[at, :] = (idx & 127).astype(F32)
            high_t[at, :] = (idx >> 7).astype(F32)
            hi = val.astype(BF).astype(F32)
            coef_hi[at, :] = hi
            coef_lo[at, :] = val - hi

    def stiff_build(begin, end):
        lanes = lax.broadcasted_iota(jnp.int32, (128, 256), 0).astype(F32).astype(BF)
        blocks = lax.broadcasted_iota(jnp.int32, (8, 256), 0).astype(F32)
        one = jnp.ones((128, 256), BF)
        none = jnp.zeros((128, 256), BF)
        third = lax.broadcasted_iota(jnp.int32, (8, 256), 1) // 80

        def some(g, carry):
            for q in range(UNROLL // 2):
                hot = []
                val = []
                s = g * UNROLL + q * 2
                for r in range(2):
                    at = pl.ds(s + r, 1)
                    low = jnp.broadcast_to(low_t[at, :], (128, 256)).astype(BF)
                    hot.append(jnp.where(low == lanes, one, none))
                    hit = jnp.broadcast_to(high_t[at, :], (8, 256)) == blocks
                    high = jnp.where(hit, coef_hi[at, :], 0.0)
                    rest = jnp.where(hit, coef_lo[at, :], 0.0)
                    for p in range(3):
                        pair = [jnp.where(third == p, high, 0.0), jnp.where(third == p, rest, 0.0)]
                        val.append(jnp.concatenate(pair, 0).astype(BF))
                out = dot(jnp.concatenate(val, 0), jnp.concatenate(hot, 0), NT)
                for r in range(2):
                    for p in range(3):
                        cut = out[(r * 3 + p) * 16 : (r * 3 + p) * 16 + 16, r * 128 : r * 128 + 128]
                        row = (p * 384 + s + r) * 8
                        tiles[pl.ds(pl.multiple_of(row, 8), 8), :] = cut[:8] + cut[8:]
            return carry

        if begin is end:
            some(begin, 0)
        else:
            lax.fori_loop(begin, end, some, 0)

    def stiff_finish():
        for r in range(4):
            for c in range(8):
                hi, lo = halves(tiles[pl.ds(c + r * 2048, 256, stride=8), :])
                stiff_hi[r * 256 : r * 256 + 256, c * 128 : c * 128 + 128] = hi
                stiff_lo[r * 256 : r * 256 + 256, c * 128 : c * 128 + 128] = lo

    def local_solve(resid, rim):
        local_buf[...] = dot_thrice(jnp.concatenate([resid, rim], 1), inv_hi[...], inv_lo[...], NT)

    def fold_basis():
        folded_hi[0:128, :] = modes_hi[:, own_cols]
        folded_lo[0:128, :] = modes_lo[:, own_cols]
        for e in range(4):
            basis_copy(e).wait_recv()
            field = dot_twice(basis_in[e], pick_t[e * 128 : (e + 1) * 128, :], NN)
            hi, lo = halves(field)
            at = slice(128 + e * 128, 256 + e * 128)
            folded_hi[at, :] = jnp.concatenate([hi, hi], 0)
            folded_lo[at, :] = jnp.concatenate([lo, lo], 0)
        lent_hi[...] = dot(folded_hi[...], pick_mat[...], NN).astype(BF)
        lent_lo[...] = dot(folded_lo[...], pick_mat[...], NN).astype(BF)

    def local_start(fold_k, resid, rim):
        local_solve(resid, rim)
        halo_start(fold_k, local_buf[:, rim_cols], 1)

    def local_finish(fold_k):
        own_buf[...] = local_buf[:, own_cols] + scatter(halo_wait(fold_k, 1))

    def nothing(*unused):
        return None

    loads[1].wait()
    rhs = rhs_ref[...]
    halo_stage(0, pick(rhs))
    stiff_prepare()
    stiff_build(0, 2)
    pl.semaphore_wait(barrier, len(greet))
    halo_send_all(0, 0)
    loads[2].wait()
    for e in range(4):
        basis_copy(e).start()
        unsent.append(lambda e=e: basis_copy(e).wait_send())

    m_hi, m_lo = halves(modes_raw[...])
    modes_hi[...] = jnp.concatenate([m_hi, m_hi], 0)
    modes_lo[...] = jnp.concatenate([m_lo, m_lo], 0)
    columns = jnp.concatenate([sends_ref[...], sends_ref[...]], 0).T
    lane_ids = lax.broadcasted_iota(jnp.int32, (128, 512), 1)
    for e in range(4):
        column = columns[:, e : e + 1]
        at = slice(e * 128, e * 128 + 128)
        hit = jnp.broadcast_to(column, (128, 512)) == lane_ids
        pick_t[at, :] = jnp.where(hit, 1.0, 0.0).astype(BF)
        for f in range(4):
            row = jnp.broadcast_to(sends_ref[f : f + 1, :], (128, 128))
            hit = jnp.broadcast_to(column, (128, 128)) == row
            gram[at, f * 128 : f * 128 + 128] = jnp.where(hit, 1.0, 0.0).astype(BF)
    stiff_build(2, 7)
    restricted = restrict(rhs, own_cols)
    rim = halo_wait(0, 0)
    def stiff_step(t):
        @pl.when(t < 3)
        def _():
            at = 6 + t
            stiff_build(at, at)

    gather_start(0, restricted + restrict(rim, rim_cols))
    loads[6].wait()
    split_into(inv_raw, inv_hi, inv_lo, 1024, 128)
    local_start(1, rhs, rim)
    gather_spread(0, stiff_step)
    loads[7].wait()
    split_into(coarse_raw, coarse_hi, coarse_lo, 256, 32)
    fold_basis()
    coarse_apply(0)
    local_finish(1)
    lent_buf[...] = pick(own_buf[...])
    stiff_build(9, 12)
    stiff_finish()
    spread = coarse_finish(0)
    halo_start(2, lent_buf[...] + dot_thrice(spread, lent_hi[...], lent_lo[...], NN), 0)
    first = own_buf[...] + dot_thrice(spread, folded_hi[...], folded_lo[...], NN)
    first_buf[...] = first

    part = dot_thrice(first, stiff_hi[:, own_cols], stiff_lo[:, own_cols], NT)
    loads[3].wait()
    diag = diag_ref[...]
    rim = halo_wait(2, 0)
    bands = part[:, rim_cols] + diag[:, rim_cols] * rim + dot_thrice(
        rim, stiff_hi[rim_cols, rim_cols], stiff_lo[rim_cols, rim_cols], NT
    )
    halo_start(3, bands, 1)
    own = part[:, own_cols] + diag[:, own_cols] * first + dot_thrice(
        rim, stiff_hi[own_cols, rim_cols], stiff_lo[own_cols, rim_cols], NT
    )
    own = rhs - own
    picked = pick(own)
    back = halo_wait(3, 1)
    halo_start(4, picked - dot_twice(back, gram[...], NN), 0)
    residual = own - scatter(back)
    res_ref[...] = residual

    restricted = restrict(residual, own_cols)
    rim = halo_wait(4, 0)
    gather_start(1, restricted + restrict(rim, rim_cols))
    local_start(5, residual, rim)
    gather_spread(1, nothing)
    coarse_apply(1)
    local_finish(5)
    base = first_buf[...] + own_buf[...]
    spread = coarse_finish(1)
    sol_ref[...] = base + dot_thrice(spread, folded_hi[...], folded_lo[...], NN)
    for finish in unsent:
        finish()


def body(
    right_side, local_inverse, modes, coarse_inverse, stiff_diag, nbr_index, nbr_coef, send_rows
):
    hbm = pl.BlockSpec(memory_space=pltpu.HBM)
    field = pltpu.VMEM((32, 512), F32)
    vmem = pl.BlockSpec(memory_space=pltpu.VMEM)
    dma = pltpu.SemaphoreType.DMA
    scratch = [
        pltpu.VMEM((32, 512), F32),
        pltpu.VMEM((1, 1024), F32),
        pltpu.VMEM((4, 128), jnp.int32),
        pltpu.VMEM((1024, 1024), F32),
        pltpu.VMEM((256, 4096), F32),
        pltpu.VMEM((64, 1024), F32),
        pltpu.VMEM((80, 1024), jnp.int32),
        pltpu.VMEM((80, 1024), F32),
        pltpu.VMEM((1024, 1024), BF),
        pltpu.VMEM((1024, 1024), BF),
        pltpu.VMEM((256, 4096), BF),
        pltpu.VMEM((256, 4096), BF),
        pltpu.VMEM((128, 1024), BF),
        pltpu.VMEM((128, 1024), BF),
        pltpu.VMEM((512, 512), BF),
        pltpu.VMEM((512, 512), BF),
        pltpu.VMEM((512, 512), BF),
        pltpu.VMEM((384, 256), F32),
        pltpu.VMEM((384, 256), F32),
        pltpu.VMEM((384, 256), F32),
        pltpu.VMEM((384, 256), F32),
        pltpu.VMEM((9216, 128), F32),
        pltpu.VMEM((1024, 1024), BF),
        pltpu.VMEM((1024, 1024), BF),
        pltpu.VMEM((64, 1024), BF),
        pltpu.VMEM((32, 512), F32),
        pltpu.VMEM((32, 512), F32),
        pltpu.VMEM((640, 512), BF),
        pltpu.VMEM((640, 512), BF),
        pltpu.VMEM((640, 512), BF),
        pltpu.VMEM((640, 512), BF),
        pltpu.VMEM((4, 64, 128), F32),
        pltpu.VMEM((2, 2, 4, 16, 128), F32),
        pltpu.VMEM((6, 4, 32, 128), F32),
        pltpu.VMEM((6, 4, 32, 128), F32),
        pltpu.VMEM((2, 64, 16, 128), F32),
        pltpu.VMEM((2, 4, 16, 128), F32),
        pltpu.VMEM((2, 4, 4, 16, 128), F32),
        pltpu.VMEM((32, 1024), F32),
        pltpu.VMEM((32, 512), F32),
        dma((8,)),
        dma((6, 4)),
        dma((6, 4)),
        dma((2, 2, 8)),
        dma((2, 2, 8)),
        dma((2, 8, 4)),
        dma((2, 8, 4)),
        dma((2, 4)),
        dma((2, 4)),
        dma((2, 2, 4)),
        dma((2, 2, 4)),
        dma((4,)),
        dma((4,)),
    ]
    return tuple(
        pl.pallas_call(
            kernel,
            out_shape=(field, field),
            in_specs=[hbm] * 8,
            out_specs=(vmem, vmem),
            scratch_shapes=scratch,
            compiler_params=pltpu.CompilerParams(
                collective_id=0, has_side_effects=True, vmem_limit_bytes=60 * 2**20
            ),
            name="schwarz",
        )(
            right_side,
            local_inverse[0, 0],
            modes[0, 0],
            coarse_inverse,
            stiff_diag[0],
            nbr_index[0, 0],
            nbr_coef[0, 0],
            send_rows[0, 0],
        )
    )


def solution(mesh):
    in_specs = (
        P(None, ("rows", "cols")),
        P("rows", "cols", None, None),
        P("rows", "cols", None, None),
        P("rows", "cols"),
        P("rows", "cols", None),
        P("rows", "cols", None, None),
        P("rows", "cols", None, None),
        P("rows", "cols", None, None),
    )
    out_specs = (P(None, ("rows", "cols")), P(None, ("rows", "cols")))
    return jax.shard_map(body, mesh=mesh, in_specs=in_specs, out_specs=out_specs, check_vma=False)
```

```python
import jax
import jax.numpy as jnp
from jax import lax
from jax.experimental import pallas as pl
from jax.experimental.pallas import tpu as pltpu
from jax.sharding import PartitionSpec as P

BF = jnp.bfloat16
F32 = jnp.float32
NT = (((1,), (1,)), ((), ()))
NN = (((1,), (0,)), ((), ()))
UNROLL = 32


def dot(a, b, dims):
    return lax.dot_general(a, b, dims, preferred_element_type=F32)


def halves(x):
    hi = x.astype(BF)
    return hi, (x - hi.astype(F32)).astype(BF)


def split_into(src, high, low, rows, step):
    def part(t, carry):
        at = pl.ds(pl.multiple_of(t * step, step), step)
        hi, lo = halves(src[at, :])
        high[at, :] = hi
        low[at, :] = lo
        return carry

    lax.fori_loop(0, rows // step, part, 0)


def dot_twice(x, w, dims):
    n = x.shape[0]
    hi, lo = halves(x)
    both = dot(jnp.concatenate([hi, lo], 0), w, dims)
    return both[:n] + both[n:]


def dot_thrice(x, high, low, dims):
    n = x.shape[0]
    hi, lo = halves(x)
    both = dot(jnp.concatenate([hi, lo], 0), high, dims)
    return both[:n] + both[n:] + dot(hi, low, dims)


def kernel(
    rhs_hbm, inv_hbm, modes_hbm, coarse_hbm, diag_hbm, index_hbm, coef_hbm, sends_hbm,
    sol_ref, res_ref,
    rhs_ref, diag_ref, sends_ref, inv_raw, coarse_raw, modes_raw, index_raw, coef_raw,
    inv_hi, inv_lo, coarse_hi, coarse_lo, modes_hi, modes_lo,
    pick_mat, pick_t, gram, low_t, high_t, coef_hi, coef_lo, tiles, stiff_hi, stiff_lo,
    x_hi, own_buf, lent_buf, folded_hi, folded_lo, lent_hi, lent_lo, basis_in, near, halo_out, halo_in, gathered, parts, others, local_buf, first_buf,
    load_sem, halo_send, halo_recv, plane_send, plane_recv, x_send, x_recv,
    col_send, col_recv, row_send, row_recv, basis_send, basis_recv,
):
    i = lax.axis_index("rows")
    j = lax.axis_index("cols")
    gx = i // 16
    gy = lax.rem(i // 8, 2)
    gz = lax.rem(i, 8)

    def row_of(x, y, z):
        return x * 16 + y * 8 + z

    loads = [
        pltpu.make_async_copy(s, d, load_sem.at[n])
        for n, (s, d) in enumerate(
            [
                (sends_hbm, sends_ref),
                (rhs_hbm, rhs_ref),
                (modes_hbm, modes_raw),
                (diag_hbm, diag_ref),
                (index_hbm, index_raw),
                (coef_hbm, coef_raw),
                (inv_hbm, inv_raw),
                (coarse_hbm, coarse_raw),
            ]
        )
    ]
    for load in loads:
        load.start()

    beside = [
        (lax.rem(i + 1, 64), j),
        (lax.rem(i + 63, 64), j),
        (i, lax.rem(j + 1, 4)),
        (i, lax.rem(j + 3, 4)),
    ]

    def plane_peer(flip, d):
        return (row_of(gx, 1 - gy if flip else gy, lax.rem(gz + d, 8)), j)

    def x_peer(d):
        return (row_of(lax.rem(gx + d, 4), gy, gz), j)

    unsent = []
    barrier = pltpu.get_barrier_semaphore()
    greet = [plane_peer(flip, d) for d in (4, 3, 5, 2, 6, 1, 7, 0) for flip in (1, 0) if flip or d]
    greet = greet + [x_peer(d) for d in (2, 1, 3)] + [(i, lax.rem(j + d, 4)) for d in (2, 1, 3)]
    greet = greet + beside[:2]
    for peer in greet:
        pl.semaphore_signal(barrier, inc=1, device_id=peer, device_id_type=pl.DeviceIdType.MESH)

    loads[0].wait()
    row_ids = lax.broadcasted_iota(jnp.int32, (512, 128), 0)
    for e in range(4):
        hit = row_ids == jnp.broadcast_to(sends_ref[e : e + 1, :], (512, 128))
        pick_mat[:, e * 128 : (e + 1) * 128] = jnp.where(hit, 1.0, 0.0).astype(BF)

    has = [i > 0, i < 63, j > 0, j < 3]

    def halo_copy(k, e, way):
        return pltpu.make_async_remote_copy(
            src_ref=halo_out.at[k, e],
            dst_ref=halo_in.at[k, e],
            send_sem=halo_send.at[k, e],
            recv_sem=halo_recv.at[k, e],
            device_id=beside[way],
            device_id_type=pl.DeviceIdType.MESH,
        )

    def halo_stage(k, values):
        for e in range(4):
            halo_out[k, e] = values[:, e * 128 : (e + 1) * 128]

    def halo_send_all(k, back):
        for e in range(4):
            halo_copy(k, e, e ^ back).start()
            unsent.append(lambda e=e: halo_copy(k, e, e ^ back).wait_send())

    def halo_start(k, values, back):
        halo_stage(k, values)
        halo_send_all(k, back)

    def halo_wait(k, back):
        got = []
        for e in range(4):
            halo_copy(k, e, e ^ back).wait_recv()
            got.append(jnp.where(has[e ^ back], halo_in[k, e], 0.0))
        return jnp.concatenate(got, 1)

    lane = lax.broadcasted_iota(jnp.int32, (16, 128), 1)
    left = lane < 64

    def pair_at(x, z):
        return pl.ds(x * 16 + z * 2, 2)

    def remote(src, dst, send, recv, peer):
        return pltpu.make_async_remote_copy(
            src_ref=src,
            dst_ref=dst,
            send_sem=send,
            recv_sem=recv,
            device_id=peer,
            device_id_type=pl.DeviceIdType.MESH,
        )

    def slot_at(y, z):
        return gx * 16 + z * 2 + y

    def plane_copy(k, flip, d, slot):
        at = gathered.at[k, pl.ds(slot, 1)]
        return remote(
            at, at, plane_send.at[k, flip, d], plane_recv.at[k, flip, d], plane_peer(flip, d)
        )

    def x_copy(k, d, dx, x):
        at = gathered.at[k, pair_at(x, lax.rem(gz - d + 8, 8))]
        return remote(at, at, x_send.at[k, d, dx], x_recv.at[k, d, dx], x_peer(dx))

    def col_copy(k, d):
        return remote(
            parts.at[k],
            others.at[k, d],
            col_send.at[k, d],
            col_recv.at[k, d],
            (i, lax.rem(j + d, 4)),
        )

    def row_copy(k, way, d):
        col = lax.rem(j + d, 4)
        return remote(
            parts.at[k, col],
            near.at[k, way, d],
            row_send.at[k, way, d],
            row_recv.at[k, way, d],
            (lax.rem(i + (1, 63)[way], 64), col),
        )

    def basis_copy(e):
        return remote(
            modes_raw.at[:, pl.ds(512 + e * 128, 128)],
            basis_in.at[e],
            basis_send.at[e],
            basis_recv.at[e],
            beside[e ^ 1],
        )

    def gather_start(k, restricted):
        mine = slot_at(gy, gz)
        block = jnp.where(left, restricted[:16], restricted[16:])
        gathered[k, pl.ds(mine, 1)] = block.reshape(1, 16, 128)
        for d in (0, 1, 7, 2, 6, 3, 5, 4):
            for flip in (1, 0):
                if flip or d:
                    plane_copy(k, flip, d, mine).start()

        def drain(d, carry):
            plane_copy(k, 0, d, mine).wait_send()
            plane_copy(k, 1, d, mine).wait_send()
            return carry

        unsent.append(lambda: lax.fori_loop(1, 8, drain, 0))
        unsent.append(lambda: plane_copy(k, 1, 0, mine).wait_send())

    def gather_spread(k, work):
        plane_copy(k, 1, 0, slot_at(1 - gy, gz)).wait_recv()
        for dx in (2, 1, 3):
            x_copy(k, 0, dx, gx).start()

        def step(t, carry):
            d = jnp.where(lax.rem(t, 2) == 1, (t + 1) // 2, 8 - t // 2)
            z = lax.rem(gz - d + 8, 8)
            plane_copy(k, 0, d, slot_at(gy, z)).wait_recv()
            plane_copy(k, 1, d, slot_at(1 - gy, z)).wait_recv()
            for dx in (2, 1, 3):
                x_copy(k, d, dx, gx).start()
            work(t)
            return carry

        lax.fori_loop(1, 8, step, 0)

        def drain(d, carry):
            for dx in range(1, 4):
                x_copy(k, d, dx, gx).wait_send()
            return carry

        unsent.append(lambda: lax.fori_loop(0, 8, drain, 0))

    def coarse_group(k, x):
        for y in range(2):
            for zz in range(4):
                a = gathered[k, x * 16 + zz * 4 + y]
                b = gathered[k, x * 16 + zz * 4 + 2 + y]
                top = jnp.where(left, a, pltpu.roll(b, 64, 1))
                low = jnp.where(left, pltpu.roll(a, 64, 1), b)
                hi, lo = halves(jnp.concatenate([top, low], 0))
                at = pl.ds((y * 4 + zz) * 128, 128)
                x_hi[0:32, at] = hi
                x_hi[32:64, at] = lo
        at = pl.ds(pl.multiple_of(x * 1024, 1024), 1024)
        both = dot(x_hi[...], coarse_hi[:, at], NT)
        return both[:32] + both[32:] + dot(x_hi[0:32, :], coarse_lo[:, at], NT)

    def coarse_apply(k):
        part = coarse_group(k, gx)
        for dx in (1, 3, 2):
            x = lax.rem(gx - dx + 4, 4)

            def arrived(d, carry, dx=dx, x=x):
                x_copy(k, d, dx, x).wait_recv()
                return carry

            lax.fori_loop(0, 8, arrived, 0)
            part = part + coarse_group(k, x)
        for c in range(4):
            a = part[:16, (c // 2) * 128 : (c // 2) * 128 + 128]
            b = part[16:, (c // 2) * 128 : (c // 2) * 128 + 128]
            if c % 2 == 0:
                packed = jnp.where(left, a, pltpu.roll(b, 64, 1))
            else:
                packed = jnp.where(left, pltpu.roll(a, 64, 1), b)
            parts[k, c] = packed
        for d in range(4):
            for way in range(2):
                row_copy(k, way, d).start()
                unsent.append(lambda way=way, d=d: row_copy(k, way, d).wait_send())
        for d in (2, 1, 3):
            col_copy(k, d).start()
            unsent.append(lambda d=d: col_copy(k, d).wait_send())

    def coarse_finish(k):
        for d in (1, 3, 2):
            col_copy(k, d).wait_recv()
        for d in range(4):
            for way in range(2):
                row_copy(k, way, d).wait_recv()

        def in_row(col):
            return parts[k, col] + others[k, 1, col] + others[k, 2, col] + others[k, 3, col]

        def in_near(way):
            return near[k, way, 0] + near[k, way, 1] + near[k, way, 2] + near[k, way, 3]

        sums = [
            in_row(j),
            jnp.where(has[1], in_near(1), 0.0),
            jnp.where(has[0], in_near(0), 0.0),
            jnp.where(has[3], in_row(lax.rem(j + 1, 4)), 0.0),
            jnp.where(has[2], in_row(lax.rem(j + 3, 4)), 0.0),
        ]
        zero = jnp.zeros((16, 128), F32)
        rows = [
            jnp.concatenate([jnp.where(left, t, zero), jnp.where(left, zero, t)], 0) for t in sums
        ]
        return jnp.concatenate(rows, 1)

    def restrict(own, cols):
        return dot_thrice(own, modes_hi[:, cols], modes_lo[:, cols], NT)

    own_cols = slice(0, 512)
    rim_cols = slice(512, 1024)

    def pick(field):
        return dot_twice(field, pick_mat[...], NN)

    def scatter(bands):
        return dot_twice(bands, pick_t[...], NN)

    def stiff_prepare():
        loads[4].wait()
        loads[5].wait()

        for t in range(3):
            def stack(raw, dtype):
                rows = [
                    raw[:, p * 384 + t * 128 : p * 384 + t * 128 + 128]
                    if p * 384 + t * 128 < 1024
                    else jnp.zeros((80, 128), dtype)
                    for p in range(3)
                ]
                rows.append(jnp.zeros((16, 128), dtype))
                return jnp.concatenate(rows, 0).T

            at = slice(t * 128, t * 128 + 128)
            idx = stack(index_raw, jnp.int32)
            val = stack(coef_raw, F32)
            low_t[at, :] = (idx & 127).astype(F32)
            high_t[at, :] = (idx >> 7).astype(F32)
            hi = val.astype(BF).astype(F32)
            coef_hi[at, :] = hi
            coef_lo[at, :] = val - hi

    def stiff_build(begin, end):
        lanes = lax.broadcasted_iota(jnp.int32, (128, 256), 0).astype(F32).astype(BF)
        blocks = lax.broadcasted_iota(jnp.int32, (8, 256), 0).astype(F32)
        one = jnp.ones((128, 256), BF)
        none = jnp.zeros((128, 256), BF)
        third = lax.broadcasted_iota(jnp.int32, (8, 256), 1) // 80

        def some(g, carry):
            for q in range(UNROLL // 2):
                hot = []
                val = []
                s = g * UNROLL + q * 2
                for r in range(2):
                    at = pl.ds(s + r, 1)
                    low = jnp.broadcast_to(low_t[at, :], (128, 256)).astype(BF)
                    hot.append(jnp.where(low == lanes, one, none))
                    hit = jnp.broadcast_to(high_t[at, :], (8, 256)) == blocks
                    high = jnp.where(hit, coef_hi[at, :], 0.0)
                    rest = jnp.where(hit, coef_lo[at, :], 0.0)
                    for p in range(3):
                        pair = [jnp.where(third == p, high, 0.0), jnp.where(third == p, rest, 0.0)]
                        val.append(jnp.concatenate(pair, 0).astype(BF))
                out = dot(jnp.concatenate(val, 0), jnp.concatenate(hot, 0), NT)
                for r in range(2):
                    for p in range(3):
                        cut = out[(r * 3 + p) * 16 : (r * 3 + p) * 16 + 16, r * 128 : r * 128 + 128]
                        row = (p * 384 + s + r) * 8
                        tiles[pl.ds(pl.multiple_of(row, 8), 8), :] = cut[:8] + cut[8:]
            return carry

        if begin is end:
            some(begin, 0)
        else:
            lax.fori_loop(begin, end, some, 0)

    def stiff_finish():
        for r in range(4):
            for c in range(8):
                hi, lo = halves(tiles[pl.ds(c + r * 2048, 256, stride=8), :])
                stiff_hi[r * 256 : r * 256 + 256, c * 128 : c * 128 + 128] = hi
                stiff_lo[r * 256 : r * 256 + 256, c * 128 : c * 128 + 128] = lo

    def local_solve(resid, rim):
        local_buf[...] = dot_thrice(jnp.concatenate([resid, rim], 1), inv_hi[...], inv_lo[...], NT)

    def fold_basis():
        folded_hi[0:128, :] = modes_hi[:, own_cols]
        folded_lo[0:128, :] = modes_lo[:, own_cols]
        for e in range(4):
            basis_copy(e).wait_recv()
            field = dot_twice(basis_in[e], pick_t[e * 128 : (e + 1) * 128, :], NN)
            hi, lo = halves(field)
            at = slice(128 + e * 128, 256 + e * 128)
            folded_hi[at, :] = jnp.concatenate([hi, hi], 0)
            folded_lo[at, :] = jnp.concatenate([lo, lo], 0)
        lent_hi[...] = dot(folded_hi[...], pick_mat[...], NN).astype(BF)
        lent_lo[...] = dot(folded_lo[...], pick_mat[...], NN).astype(BF)

    def local_start(fold_k, resid, rim):
        local_solve(resid, rim)
        halo_start(fold_k, local_buf[:, rim_cols], 1)

    def local_finish(fold_k):
        own_buf[...] = local_buf[:, own_cols] + scatter(halo_wait(fold_k, 1))

    def nothing(*unused):
        return None

    loads[1].wait()
    rhs = rhs_ref[...]
    halo_stage(0, pick(rhs))
    stiff_prepare()
    stiff_build(0, 2)
    pl.semaphore_wait(barrier, len(greet))
    halo_send_all(0, 0)
    loads[2].wait()
    for e in range(4):
        basis_copy(e).start()
        unsent.append(lambda e=e: basis_copy(e).wait_send())

    m_hi, m_lo = halves(modes_raw[...])
    modes_hi[...] = jnp.concatenate([m_hi, m_hi], 0)
    modes_lo[...] = jnp.concatenate([m_lo, m_lo], 0)
    columns = jnp.concatenate([sends_ref[...], sends_ref[...]], 0).T
    lane_ids = lax.broadcasted_iota(jnp.int32, (128, 512), 1)
    for e in range(4):
        column = columns[:, e : e + 1]
        at = slice(e * 128, e * 128 + 128)
        hit = jnp.broadcast_to(column, (128, 512)) == lane_ids
        pick_t[at, :] = jnp.where(hit, 1.0, 0.0).astype(BF)
        for f in range(4):
            row = jnp.broadcast_to(sends_ref[f : f + 1, :], (128, 128))
            hit = jnp.broadcast_to(column, (128, 128)) == row
            gram[at, f * 128 : f * 128 + 128] = jnp.where(hit, 1.0, 0.0).astype(BF)
    stiff_build(2, 7)
    restricted = restrict(rhs, own_cols)
    rim = halo_wait(0, 0)
    def stiff_step(t):
        @pl.when(t < 3)
        def _():
            at = 6 + t
            stiff_build(at, at)

    gather_start(0, restricted + restrict(rim, rim_cols))
    loads[6].wait()
    split_into(inv_raw, inv_hi, inv_lo, 1024, 128)
    local_start(1, rhs, rim)
    gather_spread(0, stiff_step)
    loads[7].wait()
    split_into(coarse_raw, coarse_hi, coarse_lo, 256, 32)
    fold_basis()
    local_finish(1)
    lent_buf[...] = pick(own_buf[...])
    coarse_apply(0)
    stiff_build(9, 12)
    stiff_finish()
    spread = coarse_finish(0)
    halo_start(2, lent_buf[...] + dot_thrice(spread, lent_hi[...], lent_lo[...], NN), 0)
    first = own_buf[...] + dot_thrice(spread, folded_hi[...], folded_lo[...], NN)
    first_buf[...] = first

    part = dot_thrice(first, stiff_hi[:, own_cols], stiff_lo[:, own_cols], NT)
    loads[3].wait()
    diag = diag_ref[...]
    rim = halo_wait(2, 0)
    bands = part[:, rim_cols] + diag[:, rim_cols] * rim + dot_thrice(
        rim, stiff_hi[rim_cols, rim_cols], stiff_lo[rim_cols, rim_cols], NT
    )
    halo_start(3, bands, 1)
    own = part[:, own_cols] + diag[:, own_cols] * first + dot_thrice(
        rim, stiff_hi[own_cols, rim_cols], stiff_lo[own_cols, rim_cols], NT
    )
    own = rhs - own
    picked = pick(own)
    back = halo_wait(3, 1)
    halo_start(4, picked - dot_twice(back, gram[...], NN), 0)
    residual = own - scatter(back)
    res_ref[...] = residual

    restricted = restrict(residual, own_cols)
    rim = halo_wait(4, 0)
    gather_start(1, restricted + restrict(rim, rim_cols))
    local_start(5, residual, rim)
    gather_spread(1, nothing)
    coarse_apply(1)
    local_finish(5)
    base = first_buf[...] + own_buf[...]
    spread = coarse_finish(1)
    sol_ref[...] = base + dot_thrice(spread, folded_hi[...], folded_lo[...], NN)
    for finish in unsent:
        finish()


def body(
    right_side, local_inverse, modes, coarse_inverse, stiff_diag, nbr_index, nbr_coef, send_rows
):
    hbm = pl.BlockSpec(memory_space=pltpu.HBM)
    field = pltpu.VMEM((32, 512), F32)
    vmem = pl.BlockSpec(memory_space=pltpu.VMEM)
    dma = pltpu.SemaphoreType.DMA
    scratch = [
        pltpu.VMEM((32, 512), F32),
        pltpu.VMEM((1, 1024), F32),
        pltpu.VMEM((4, 128), jnp.int32),
        pltpu.VMEM((1024, 1024), F32),
        pltpu.VMEM((256, 4096), F32),
        pltpu.VMEM((64, 1024), F32),
        pltpu.VMEM((80, 1024), jnp.int32),
        pltpu.VMEM((80, 1024), F32),
        pltpu.VMEM((1024, 1024), BF),
        pltpu.VMEM((1024, 1024), BF),
        pltpu.VMEM((256, 4096), BF),
        pltpu.VMEM((256, 4096), BF),
        pltpu.VMEM((128, 1024), BF),
        pltpu.VMEM((128, 1024), BF),
        pltpu.VMEM((512, 512), BF),
        pltpu.VMEM((512, 512), BF),
        pltpu.VMEM((512, 512), BF),
        pltpu.VMEM((384, 256), F32),
        pltpu.VMEM((384, 256), F32),
        pltpu.VMEM((384, 256), F32),
        pltpu.VMEM((384, 256), F32),
        pltpu.VMEM((9216, 128), F32),
        pltpu.VMEM((1024, 1024), BF),
        pltpu.VMEM((1024, 1024), BF),
        pltpu.VMEM((64, 1024), BF),
        pltpu.VMEM((32, 512), F32),
        pltpu.VMEM((32, 512), F32),
        pltpu.VMEM((640, 512), BF),
        pltpu.VMEM((640, 512), BF),
        pltpu.VMEM((640, 512), BF),
        pltpu.VMEM((640, 512), BF),
        pltpu.VMEM((4, 64, 128), F32),
        pltpu.VMEM((2, 2, 4, 16, 128), F32),
        pltpu.VMEM((6, 4, 32, 128), F32),
        pltpu.VMEM((6, 4, 32, 128), F32),
        pltpu.VMEM((2, 64, 16, 128), F32),
        pltpu.VMEM((2, 4, 16, 128), F32),
        pltpu.VMEM((2, 4, 4, 16, 128), F32),
        pltpu.VMEM((32, 1024), F32),
        pltpu.VMEM((32, 512), F32),
        dma((8,)),
        dma((6, 4)),
        dma((6, 4)),
        dma((2, 2, 8)),
        dma((2, 2, 8)),
        dma((2, 8, 4)),
        dma((2, 8, 4)),
        dma((2, 4)),
        dma((2, 4)),
        dma((2, 2, 4)),
        dma((2, 2, 4)),
        dma((4,)),
        dma((4,)),
    ]
    return tuple(
        pl.pallas_call(
            kernel,
            out_shape=(field, field),
            in_specs=[hbm] * 8,
            out_specs=(vmem, vmem),
            scratch_shapes=scratch,
            compiler_params=pltpu.CompilerParams(
                collective_id=0, has_side_effects=True, vmem_limit_bytes=60 * 2**20
            ),
            name="schwarz",
        )(
            right_side,
            local_inverse[0, 0],
            modes[0, 0],
            coarse_inverse,
            stiff_diag[0],
            nbr_index[0, 0],
            nbr_coef[0, 0],
            send_rows[0, 0],
        )
    )


def solution(mesh):
    in_specs = (
        P(None, ("rows", "cols")),
        P("rows", "cols", None, None),
        P("rows", "cols", None, None),
        P("rows", "cols"),
        P("rows", "cols", None),
        P("rows", "cols", None, None),
        P("rows", "cols", None, None),
        P("rows", "cols", None, None),
    )
    out_specs = (P(None, ("rows", "cols")), P(None, ("rows", "cols")))
    return jax.shard_map(body, mesh=mesh, in_specs=in_specs, out_specs=out_specs, check_vma=False)
```
